256 devices in a mesh: slab: 64 (over z, x, core), own: 4 (over y).
Axes of the slice: x: 4, y: 4, z: 8, core: 2. Of those that a mesh axis runs over, the one named last changes fastest.
Arguments:
- src_factor: float32 [256, 131072], P('own', 'slab'), may hold values from -5 to 5
- dst_factor: float32 [256, 131072], P('own', 'slab'), may hold values from -5 to 5
- hour_factor: float32 [512, 256], P('slab', 'own'), may hold values from 0.5 to 2
- tile_src: int32 [1920], P('slab'), may hold values from 0 to 1023, as said below
- tile_dst: int32 [1920], P('slab'), may hold values from 0 to 1023, as said below
- tile_hour: int32 [1920], P('slab'), may hold values from 0 to 511, as said below
- tile_count: int32 [64], P('slab'), may hold values from 2 to 30, as said below
- src_place: int32 [1024], replicated, may hold values from 0 to 1023, as said below
- dst_place: int32 [1024], replicated, may hold values from 0 to 1023, as said below
- tile_bits: int32 [1920, 8, 128], P('slab'), may hold values from 0 to 65535
Outputs:
- grad_src: float32 [256, 131072], P('own', 'slab')
- grad_dst: float32 [256, 131072], P('own', 'slab')
- grad_hour: float32 [512, 256], P('slab', 'own')
The draws below stay inside these ranges and needn't reach their ends.
Inputs may be any that keep to these rules, and one draw needn't show every extreme that they name: `tile_src`: slots s * 30 to s * 30 + 29 form slab group s. Among one group's slots, padded ones included, the source blocks whose storage position lies on one storage slab index (src_place[id] // 16) are at most 2 different ones; every group has a storage slab index with 2. `tile_dst`: the same holds for destination blocks with dst_place. `tile_hour`: A tile of slab group s has an hour of s * 8 to s * 8 + 7. `tile_count`: some group fills all 30 slots, some has 2 live tiles. `src_place`: A permutation of the block ids. `dst_place`: A permutation of the block ids.
All inputs are finite; a program needn't handle non-finite values.
Results may differ from the reference program's by a relative error of at most 0.0003.
Values sent between devices are 32-bit elements; how exact they have to be, the bound alone decides.
No kernel may reach another device: no remote copies, remote signals or barrier semaphores. Data moves between devices by JAX's collectives and lax.ppermute only.
A program may use at most 64 MiB of HBM per device.

```python
import math
import jax
import jax.numpy as jnp
from jax import lax

RANK = 256
BLOCK = 128
CAP = 2
TILE_CAP = 30
BLK_DEV = 16
HOUR_DEV = 8
GROUPS = 64
TILES = 1920
NBLK = 1024
ROWS = 131072
HOURS = 512
WORDS = 8


def placement_table(key, salt):
    return jax.random.permutation(jax.random.fold_in(key, salt), NBLK).astype(jnp.int32)


def draw_src_place(key, part):
    return placement_table(key, 11)


def draw_dst_place(key, part):
    return placement_table(key, 12)


def tile_blocks(key, salt, place_salt):
    place = placement_table(key, place_salt)
    inverse = jnp.argsort(place, stable=True).astype(jnp.int32)
    base = jax.random.fold_in(key, salt)
    key_owner, key_which, key_first = jax.random.split(base, 3)
    owner = jax.random.randint(key_owner, (GROUPS, TILE_CAP), 0, GROUPS)
    which = jax.random.randint(key_which, (GROUPS, TILE_CAP), 0, CAP)
    first = jax.random.randint(key_first, (GROUPS, GROUPS), 0, BLK_DEV)
    owner = owner.at[:, 1].set(owner[:, 0])
    which = which.at[:, 0].set(0).at[:, 1].set(1)
    group_rows = jnp.arange(GROUPS, dtype=jnp.int32)[:, None]
    start = first[group_rows, owner]
    within = (start + which * (BLK_DEV // CAP)) % BLK_DEV
    storage = owner * BLK_DEV + within
    return inverse[storage].reshape(-1).astype(jnp.int32)


def draw_tile_src(key, part):
    return tile_blocks(key, 21, 11)


def draw_tile_dst(key, part):
    return tile_blocks(key, 22, 12)


def draw_tile_hour(key, part):
    offsets = jax.random.randint(jax.random.fold_in(key, 41), (GROUPS, TILE_CAP), 0, HOUR_DEV)
    offsets = offsets.at[:, 0].set(0).at[:, 2].set(HOUR_DEV - 1)
    group_rows = jnp.arange(GROUPS, dtype=jnp.int32)[:, None]
    return (group_rows * HOUR_DEV + offsets).reshape(-1).astype(jnp.int32)


def draw_tile_count(key, part):
    key_counts, key_top = jax.random.split(jax.random.fold_in(key, 31))
    counts = jax.random.randint(key_counts, (GROUPS,), TILE_CAP // 2, TILE_CAP + 1)
    heaviest = jax.random.randint(key_top, (), 0, GROUPS)
    counts = counts.at[heaviest].set(TILE_CAP)
    counts = counts.at[(heaviest + 1) % GROUPS].set(2)
    return counts.astype(jnp.int32)


def touch_ends(array, stream_key, least, high):
    longest = array.shape.index(max(array.shape))
    spots = []
    for shift in (0, 1):
        where = [jax.random.randint(jax.random.fold_in(stream_key, axis), (), 0, length) for axis, length in enumerate(array.shape)]
        where[longest] = (where[longest] + shift) % array.shape[longest]
        spots.append(tuple(where))
    return array.at[spots[0]].set(least).at[spots[1]].set(high)


def block_scale(rng, shape, pieces, least, largest):
    loudness, own = 1.0, jax.random.fold_in(rng, 6)
    for dim, parts in pieces:
        heights = jnp.exp(jax.random.uniform(jax.random.fold_in(own, dim), (parts,), jnp.float32, least / len(pieces), largest / len(pieces)))
        loudness = loudness * jnp.repeat(heights, shape[dim] // parts).reshape([-1 if axis == dim else 1 for axis in range(len(shape))])
    return loudness


def centred(stream_key, extent, deviation, limit, shards=(), held_as=jnp.bfloat16):
    values = jax.random.normal(stream_key, extent, jnp.float32) * deviation
    if len(shards) > 0:
        values = block_scale(stream_key, extent, shards, -0.22, 0.18) * values
    return jnp.clip(values, min=-limit, max=limit).astype(held_as)


def setup_inputs(seed: int = 0) -> dict:
    keys = jax.random.split(jax.random.key(seed), 11)
    src_factor = centred(keys[0], (RANK, ROWS), 0.35, 5.0, ((0, 4), (1, 64)), jnp.float32)
    dst_factor = centred(keys[1], (RANK, ROWS), 0.35, 5.0, ((0, 4), (1, 64)), jnp.float32)
    hour_factor = jnp.clip(jnp.exp(math.log(2.0) - 1.3862944 * jax.random.uniform(keys[2], (HOURS, RANK), jnp.float32) ** block_scale(keys[2], (HOURS, RANK), ((0, 64), (1, 4)), -0.2, 0.2)), 0.5, 2.0)
    tile_src = draw_tile_src(jax.random.fold_in(keys[10], 71), 0)
    tile_dst = draw_tile_dst(jax.random.fold_in(keys[10], 71), 0)
    tile_hour = draw_tile_hour(jax.random.fold_in(keys[10], 71), 0)
    tile_count = draw_tile_count(jax.random.fold_in(keys[10], 71), 0)
    src_place = draw_src_place(jax.random.fold_in(keys[10], 71), 0)
    dst_place = draw_dst_place(jax.random.fold_in(keys[10], 71), 0)
    tile_bits = touch_ends(jax.random.randint(keys[9], (TILES, WORDS, BLOCK), 0, 65536), jax.random.fold_in(keys[9], 1), 0, 65535).astype(jnp.int32)
    return dict(src_factor=src_factor, dst_factor=dst_factor, hour_factor=hour_factor, tile_src=tile_src, tile_dst=tile_dst, tile_hour=tile_hour, tile_count=tile_count, src_place=src_place, dst_place=dst_place, tile_bits=tile_bits)


precise = lax.Precision.HIGHEST


def unpack_tile(packed):
    shifts = jnp.arange(16, dtype=jnp.int32)
    bit_values = jnp.right_shift(packed[:, None, :], shifts[None, :, None]) & 1
    return bit_values.reshape(packed.shape[0] * 16, packed.shape[1]).astype(jnp.float32)


def reference(src_factor, dst_factor, hour_factor, tile_src, tile_dst, tile_hour, tile_count, src_place, dst_place, tile_bits):
    src_blocks = jnp.transpose(src_factor.reshape(RANK, NBLK, BLOCK), (1, 2, 0))
    dst_blocks = jnp.transpose(dst_factor.reshape(RANK, NBLK, BLOCK), (1, 2, 0))
    start_state = (jnp.zeros((NBLK, BLOCK, RANK), jnp.float32),
                   jnp.zeros((NBLK, BLOCK, RANK), jnp.float32),
                   jnp.zeros((HOURS, RANK), jnp.float32))

    def group_step(state, group):
        def tile_step(slot, inner):
            grad_src, grad_dst, grad_hour = inner
            index = (group * TILE_CAP + slot).astype(jnp.int32)
            src_at = src_place[tile_src[index]]
            dst_at = dst_place[tile_dst[index]]
            hour_at = tile_hour[index]
            src_tile = src_blocks[src_at]
            dst_tile = dst_blocks[dst_at]
            hour_row = hour_factor[hour_at]
            logits = jnp.dot(src_tile * hour_row[None, :], dst_tile.T, precision=precise)
            residual = jax.nn.sigmoid(logits) - unpack_tile(tile_bits[index])
            along_dst = jnp.dot(residual, dst_tile, precision=precise)
            along_src = jnp.dot(residual.T, src_tile, precision=precise)
            grad_src = grad_src.at[src_at].add(along_dst * hour_row[None, :])
            grad_dst = grad_dst.at[dst_at].add(along_src * hour_row[None, :])
            grad_hour = grad_hour.at[hour_at].add(jnp.sum(src_tile * along_dst, axis=0))
            return grad_src, grad_dst, grad_hour
        return lax.fori_loop(0, tile_count[group], tile_step, state), None

    final_state, unused = lax.scan(group_step, start_state, jnp.arange(GROUPS, dtype=jnp.int32))
    grad_src, grad_dst, grad_hour = final_state
    return grad_src.reshape(ROWS, RANK).T, grad_dst.reshape(ROWS, RANK).T, grad_hour
```

```python
import jax
import jax.numpy as jnp
from jax import lax
from jax.experimental import pallas as pl
from jax.experimental.pallas import tpu as pltpu
from jax.sharding import Mesh, PartitionSpec as P

NZ, NX, NC, NO = 8, 4, 2, 4
SLAB = ("z", "x", "c")
GROUPS = 64
TILE_CAP = 30
SIDE = 128
RK = 64
STORED = 16
SLOTS = 5
ROWS = 3 * SLOTS + 1
PER = 10
ROUND = PER * NO
VMEM = pl.BlockSpec(memory_space=pltpu.VMEM)
SMEM = pl.BlockSpec(memory_space=pltpu.SMEM)
f32, bf16, i32 = jnp.float32, jnp.bfloat16, jnp.int32
PARAMS = pltpu.CompilerParams(vmem_limit_bytes=48 * 1024 * 1024)


def lane_block(within):
    return pl.ds(pl.multiple_of(within * SIDE, SIDE), SIDE)


def split(x):
    hi = x.astype(bf16)
    return hi, (x - hi.astype(f32)).astype(bf16)


def dot3(a, b, dims):
    dg = lambda p, q: lax.dot_general(p, q, (dims, ((), ())), preferred_element_type=f32)
    return dg(a[0], b[0]) + (dg(a[0], b[1]) + dg(a[1], b[0]))


def as_column(row):
    return jnp.broadcast_to(row, (SIDE, RK)).T


def send_kernel(scal, src_ids, dst_ids, hours, src_place, dst_place, bits, hour_rows, out, where, count):
    own, first_hour, live, pair_round = scal[0], scal[1], scal[2], scal[3]

    @pl.loop(0, GROUPS)
    def _(g):
        count[g] = 0

    out[...] = jnp.zeros_like(out)
    lane = lax.broadcasted_iota(i32, (1, SIDE), 1)

    def step(t, hist):
        src_at = src_place[src_ids[t]]
        dst_at = dst_place[dst_ids[t]]
        to = (src_at // 128) * 8 + (dst_at // STORED) % 8
        rank = count[to]
        slot = rank - pair_round * SLOTS
        here = (t < live) & (slot >= 0) & (slot < SLOTS)
        where[t] = jnp.where(here, to * 8 + slot, -1)

        @pl.when(t < live)
        def _():
            count[to] = rank + 1

        @pl.when(here)
        def _():
            for i in range(2):
                out[to, pl.ds(3 * slot + i, 1), :] = bits[t, pl.ds(2 * own + i, 1), :].astype(f32)
            c = hour_rows[pl.ds(hours[t] - first_hour, 1), :]
            row = jnp.concatenate([c, jnp.zeros_like(c)], axis=1)
            row = jnp.where(lane == 64, 1.0, row)
            row = jnp.where(lane == 65, src_at.astype(f32), row)
            row = jnp.where(lane == 66, dst_at.astype(f32), row)
            out[to, pl.ds(3 * slot + 2, 1), :] = row

        return hist + jnp.where((lane == to) & (t < live), 1.0, 0.0)

    hist = lax.fori_loop(0, TILE_CAP, step, jnp.zeros((1, SIDE), f32))
    out[:, ROWS - 1 : ROWS, :] = jnp.broadcast_to(hist[None], (GROUPS, 1, SIDE))


def plan_kernel(scal, meta, recv, a00, a10, a30, a2t0, a2b0, a01, a11, a31, a2t1, a2b1, lst, *outs):
    own, x_at, c_at, base = scal[0], scal[1], scal[2], scal[3]

    def scan(i, n):
        pos = n - base
        valid = meta[3 * i]

        @pl.when((valid == 1) & (pos >= 0) & (pos < ROUND))
        def _():
            lst[pos] = meta[3 * i + 1]
            lst[ROUND + pos] = meta[3 * i + 2]
            lst[2 * ROUND + pos] = i

        return n + valid

    total = lax.fori_loop(0, GROUPS * SLOTS, scan, 0)
    n = jnp.clip(total - base, 0, ROUND)
    lst[3 * ROUND] = n
    sources = {
        (0, 0): (a00,), (1, 0): (a10,), (2, 0): (a2t0, a2b0), (3, 0): (a30,),
        (0, 1): (a01,), (1, 1): (a11,), (2, 1): (a2t1, a2b1), (3, 1): (a31,),
    }
    for d in range(NO):
        to = (own + d) % NO

        @pl.loop(0, (n - to + NO - 1) // NO)
        def _(j):
            k = NO * j + to
            src_at = lst[k]
            slot = lst[2 * ROUND + k]
            w = (src_at // STORED) % 8
            cols = lane_block(src_at % STORED)
            dx = (w // 2 - x_at + NX) % NX
            dc = (w % 2 + c_at) % 2
            row = (slot // SLOTS) * ROWS + 3 * (slot % SLOTS) + 2
            c = as_column(recv[pl.ds(row, 1), :RK])
            for (sx, sc), refs in sources.items():

                @pl.when((dx == sx) & (dc == sc))
                def _():
                    step = RK // len(refs)
                    for h, ref in enumerate(refs):
                        outs[d][j, h * step : (h + 1) * step, :] = (
                            ref[:, cols] * c[h * step : (h + 1) * step]
                        )


def pack_kernel(scal, lst, recv, b, *outs):
    own = scal[0]
    n = lst[3 * ROUND]
    for d in range(NO):
        to = (own + d) % NO

        @pl.loop(0, (n - to + NO - 1) // NO)
        def _(j):
            k = NO * j + to
            dst_at = lst[ROUND + k]
            slot = lst[2 * ROUND + k]
            row = (slot // SLOTS) * ROWS + 3 * (slot % SLOTS)
            outs[d][j, :RK, :] = b[dst_at // 128, :, lane_block(dst_at % STORED)]
            for i in range(2):
                outs[d][j, RK + i : RK + i + 1, :] = recv[pl.ds(row + i, 1), :]


def tile_kernel(scal, lst, a0, a1, a2, a3, b0, b1, b2, b3, u0, u1, u2, u3, g0, g1, g2, g3, res):
    own = scal[0]
    n = lst[3 * ROUND]
    a_in, b_in, u_out, g_out = (a0, a1, a2, a3), (b0, b1, b2, b3), (u0, u1, u2, u3), (g0, g1, g2, g3)
    shift = lax.broadcasted_iota(i32, (32, SIDE), 0) % 16

    @pl.loop(0, (n - own + NO - 1) // NO)
    def _(j):
        a = split(jnp.concatenate([r[j] for r in a_in], axis=0))
        b = split(jnp.concatenate([r[j, :RK] for r in b_in], axis=0))
        res[...] = dot3(a, b, ((0,), (0,)))
        for d in range(NO):
            rows = pl.ds(pl.multiple_of(((own - d + NO) % NO) * 32, 32), 32)
            words = jnp.concatenate(
                [jnp.broadcast_to(b_in[d][j, RK + i : RK + i + 1, :], (16, SIDE)) for i in range(2)], axis=0
            ).astype(i32)
            entries = (jnp.right_shift(words, shift) & 1).astype(f32)
            res[rows, :] = jax.nn.sigmoid(res[rows, :]) - entries
        r = split(res[...])
        u = dot3(b, r, ((1,), (1,)))
        g = dot3(a, r, ((1,), (0,)))
        for d in range(NO):
            u_out[d][j] = u[RK * d : RK * (d + 1)]
            g_out[d][j] = g[RK * d : RK * (d + 1)]


def dst_sum_kernel(scal, lst, g0, g1, g2, g3, out):
    own = scal[0]
    n = lst[3 * ROUND]
    out[...] = jnp.zeros_like(out)
    for d, g in enumerate((g0, g1, g2, g3)):
        to = (own + d) % NO

        @pl.loop(0, (n - to + NO - 1) // NO)
        def _(j):
            dst_at = lst[ROUND + NO * j + to]
            cols = lane_block(dst_at % STORED)
            out[dst_at // 128, :, cols] += g[j]


def src_sum_kernel(
    scal, lst, recv, u0, u1, u2, u3, a00, a10, a30, a2t0, a2b0, a01, a11, a31, a2t1, a2b1, keep, give, hour, a_tile
):
    own, x_at, c_at = scal[0], scal[1], scal[2]
    n = lst[3 * ROUND]
    keep[...] = jnp.zeros_like(keep)
    give[...] = jnp.zeros_like(give)
    hour[...] = jnp.zeros_like(hour)
    sources = {
        (0, 0): (a00,), (1, 0): (a10,), (2, 0): (a2t0, a2b0), (3, 0): (a30,),
        (0, 1): (a01,), (1, 1): (a11,), (2, 1): (a2t1, a2b1), (3, 1): (a31,),
    }
    for d, u in enumerate((u0, u1, u2, u3)):
        to = (own + d) % NO

        @pl.loop(0, (n - to + NO - 1) // NO)
        def _(j):
            k = NO * j + to
            src_at = lst[k]
            slot = lst[2 * ROUND + k]
            w = (src_at // STORED) % 8
            cols = lane_block(src_at % STORED)
            dx = (w // 2 - x_at + NX) % NX
            dc = (w % 2 + c_at) % 2
            g_at, s_at = slot // SLOTS, slot % SLOTS
            c = as_column(recv[pl.ds(g_at * ROWS + 3 * s_at + 2, 1), :RK])
            part = u[j]
            term = c * part
            for (sx, sc), refs in sources.items():

                @pl.when((dx == sx) & (dc == sc))
                def _():
                    step = RK // len(refs)
                    for h, ref in enumerate(refs):
                        a_tile[h * step : (h + 1) * step, :] = ref[:, cols]
                    total = give if sc else keep
                    total[sx, :, cols] += term

            row = lax.dot_general(
                jnp.ones((8, SIDE), f32), a_tile[...] * part, (((1,), (1,)), ((), ())),
                precision=lax.Precision.HIGHEST, preferred_element_type=f32,
            )
            hour[g_at, pl.ds(s_at, 1), :RK] = row[:1]


def hour_kernel(scal, hours, where, back, out):
    first_hour = scal[1]
    out[...] = jnp.zeros_like(out)

    @pl.loop(0, TILE_CAP)
    def _(t):
        at = where[t]

        @pl.when(at >= 0)
        def _():
            h = hours[t] - first_hour
            out[pl.ds(h, 1), :] += back[at // 8, pl.ds(at % 8, 1), :RK]


def shape(*dims, dtype=f32):
    return jax.ShapeDtypeStruct(dims, dtype)


def call(kernel, out_shape, in_specs, args, out_specs=None, scratch=()):
    if out_specs is None:
        out_specs = jax.tree.map(lambda _: VMEM, out_shape)
    return pl.pallas_call(
        kernel, out_shape=out_shape, in_specs=in_specs, out_specs=out_specs,
        scratch_shapes=scratch, compiler_params=PARAMS,
    )(*args)


def hop(value, axis, size, by):
    return lax.ppermute(value, axis, [(i, (i + by) % size) for i in range(size)])


def per_device(
    src_factor, dst_factor, hour_factor, tile_src, tile_dst, tile_hour, tile_count, src_place, dst_place, tile_bits
):
    z_at, x_at, c_at, own = (lax.axis_index(n).astype(i32) for n in ("z", "x", "c", "own"))
    first_hour = ((z_at * NX + x_at) * NC + c_at) * hour_factor.shape[0]
    live = tile_count[0]
    half = RK // 2

    with jax.named_scope("gather_dst"):
        b_all = lax.all_gather(dst_factor, "z", axis=0)
    with jax.named_scope("gather_src"):
        up = hop(src_factor, "x", NX, 1)
        down = hop(src_factor, "x", NX, -1)
        far_top = hop(up[:half], "x", NX, 1)
        far_bottom = hop(down[half:], "x", NX, -1)
        mine = (src_factor, down, up, far_top, far_bottom)
        a_all = mine + tuple(hop(v, "c", NC, 1) for v in mine)

    def one_round(pair_round, base):
        with jax.named_scope("slots"):
            scal = jnp.stack([own, first_hour, live, pair_round])
            sent, where = call(
                send_kernel, (shape(GROUPS, ROWS, SIDE), shape(TILE_CAP, dtype=i32)),
                [SMEM] * 6 + [VMEM] * 2,
                (scal, tile_src, tile_dst, tile_hour, src_place, dst_place, tile_bits, hour_factor),
                out_specs=(VMEM, SMEM), scratch=[pltpu.SMEM((GROUPS,), i32)],
            )
            got = lax.all_to_all(sent, SLAB, 0, 0)
            meta = got[:, 2 : ROWS - 1 : 3, RK : RK + 3].astype(i32).reshape(-1)
            rows = got.reshape(GROUPS * ROWS, SIDE)
            hist = got[:, ROWS - 1, :GROUPS].astype(i32)
        at = jnp.stack([own, x_at, c_at, base])
        with jax.named_scope("src_exchange"):
            lst, *a_out = call(
                plan_kernel, (shape(3 * ROUND + 8, dtype=i32),) + (shape(PER, RK, SIDE),) * NO,
                [SMEM] * 2 + [VMEM] * 11, (at, meta, rows) + a_all, out_specs=(SMEM,) + (VMEM,) * NO,
            )
            a_in = [v if d == 0 else hop(v, "own", NO, d) for d, v in enumerate(a_out)]
        with jax.named_scope("dst_exchange"):
            b_out = call(
                pack_kernel, (shape(PER, RK + 8, SIDE),) * NO, [SMEM] * 2 + [VMEM] * 2, (at, lst, rows, b_all)
            )
            b_in = [v if d == 0 else hop(v, "own", NO, d) for d, v in enumerate(b_out)]
        with jax.named_scope("tiles"):
            parts = call(
                tile_kernel, (shape(PER, RK, SIDE),) * (2 * NO), [SMEM] * 2 + [VMEM] * 8,
                (at, lst, *a_in, *b_in), scratch=[pltpu.VMEM((SIDE, SIDE), f32)],
            )
        with jax.named_scope("dst_back"):
            g = [v if d == 0 else hop(v, "own", NO, -d) for d, v in enumerate(parts[NO:])]
            g_sum = call(dst_sum_kernel, shape(NZ, RK, STORED * SIDE), [SMEM] * 2 + [VMEM] * NO, (at, lst, *g))
            grad_dst = lax.psum_scatter(g_sum, "z", scatter_dimension=0)
        with jax.named_scope("src_back"):
            u = [v if d == 0 else hop(v, "own", NO, -d) for d, v in enumerate(parts[:NO])]
            keep, give, hour_terms = call(
                src_sum_kernel,
                (shape(NX, RK, STORED * SIDE), shape(NX, RK, STORED * SIDE), shape(GROUPS, 8, SIDE)),
                [SMEM] * 2 + [VMEM] * 15, (at, lst, rows, *u) + a_all, scratch=[pltpu.VMEM((RK, SIDE), f32)],
            )
            s = keep + hop(give, "c", NC, 1)
            top = hop(s[2, :half], "x", NX, 1)
            bottom = hop(s[2, half:], "x", NX, -1)
            one = hop(jnp.concatenate([s[1, :half] + top, s[1, half:]]), "x", NX, 1)
            three = hop(jnp.concatenate([s[3, :half], s[3, half:] + bottom]), "x", NX, -1)
            grad_src = s[0] + one + three
        with jax.named_scope("hours"):
            back = lax.all_to_all(hour_terms, SLAB, 0, 0)
            grad_hour = call(
                hour_kernel, shape(*hour_factor.shape), [SMEM] * 3 + [VMEM], (scal, tile_hour, where, back)
            )
        return (grad_src, grad_dst, grad_hour), hist

    zero = jnp.zeros((), i32)
    grads, hist = one_round(zero, zero)

    def busiest(pair_round):
        return jnp.max(jnp.sum(jnp.clip(hist - pair_round * SLOTS, 0, SLOTS), axis=0))

    def following(pair_round, base):
        more = base + ROUND < busiest(pair_round)
        return jnp.where(more, pair_round, pair_round + 1), jnp.where(more, base + ROUND, 0)

    def body(state):
        pair_round, base, sums = state
        terms, _ = one_round(pair_round, base)
        return following(pair_round, base) + (jax.tree.map(jnp.add, sums, terms),)

    last = lax.while_loop(lambda state: jnp.max(hist) > state[0] * SLOTS, body, following(zero, zero) + (grads,))
    return last[2]


def solution(mesh):
    fine = Mesh(mesh.devices.reshape(NZ, NX, NC, NO), SLAB + ("own",))
    return jax.shard_map(
        per_device,
        mesh=fine,
        in_specs=(
            P("own", SLAB), P("own", SLAB), P(SLAB, "own"), P(SLAB), P(SLAB), P(SLAB), P(SLAB), P(), P(),
            P(SLAB, None, None),
        ),
        out_specs=(P("own", SLAB), P("own", SLAB), P(SLAB, "own")),
        check_vma=False,
    )
```

```python
import jax
import jax.numpy as jnp
from jax import lax
from jax.experimental import pallas as pl
from jax.experimental.pallas import tpu as pltpu
from jax.sharding import Mesh, PartitionSpec as P

NZ, NX, NC, NO = 8, 4, 2, 4
SLAB = ("z", "x", "c")
GROUPS = 64
TILE_CAP = 30
SIDE = 128
RK = 64
STORED = 16
SLOTS = 5
ROWS = 3 * SLOTS + 1
PER = 10
ROUND = PER * NO
VMEM = pl.BlockSpec(memory_space=pltpu.VMEM)
SMEM = pl.BlockSpec(memory_space=pltpu.SMEM)
ANY = pl.BlockSpec(memory_space=pl.ANY)
f32, bf16, i32 = jnp.float32, jnp.bfloat16, jnp.int32
PARAMS = pltpu.CompilerParams(vmem_limit_bytes=48 * 1024 * 1024)


def lane_block(within):
    return pl.ds(pl.multiple_of(within * SIDE, SIDE), SIDE)


def split(x):
    hi = x.astype(bf16)
    return hi, (x - hi.astype(f32)).astype(bf16)


def dot3(a, b, dims):
    dg = lambda p, q: lax.dot_general(p, q, (dims, ((), ())), preferred_element_type=f32)
    return dg(a[0], b[0]) + (dg(a[0], b[1]) + dg(a[1], b[0]))


def as_column(row):
    return jnp.broadcast_to(row, (SIDE, RK)).T


def send_kernel(scal, src_ids, dst_ids, hours, src_place, dst_place, bits, hour_rows, out, where, count):
    own, first_hour, live, pair_round = scal[0], scal[1], scal[2], scal[3]

    @pl.loop(0, GROUPS)
    def _(g):
        count[g] = 0

    out[...] = jnp.zeros_like(out)
    lane = lax.broadcasted_iota(i32, (1, SIDE), 1)

    def step(t, hist):
        src_at = src_place[src_ids[t]]
        dst_at = dst_place[dst_ids[t]]
        to = (src_at // 128) * 8 + (dst_at // STORED) % 8
        rank = count[to]
        slot = rank - pair_round * SLOTS
        here = (t < live) & (slot >= 0) & (slot < SLOTS)
        where[t] = jnp.where(here, to * 8 + slot, -1)

        @pl.when(t < live)
        def _():
            count[to] = rank + 1

        @pl.when(here)
        def _():
            for i in range(2):
                out[to, pl.ds(3 * slot + i, 1), :] = bits[t, pl.ds(2 * own + i, 1), :].astype(f32)
            c = hour_rows[pl.ds(hours[t] - first_hour, 1), :]
            row = jnp.concatenate([c, jnp.zeros_like(c)], axis=1)
            row = jnp.where(lane == 64, 1.0, row)
            row = jnp.where(lane == 65, src_at.astype(f32), row)
            row = jnp.where(lane == 66, dst_at.astype(f32), row)
            out[to, pl.ds(3 * slot + 2, 1), :] = row

        return hist + jnp.where((lane == to) & (t < live), 1.0, 0.0)

    hist = lax.fori_loop(0, TILE_CAP, step, jnp.zeros((1, SIDE), f32))
    out[:, ROWS - 1 : ROWS, :] = jnp.broadcast_to(hist[None], (GROUPS, 1, SIDE))


def list_kernel(scal, meta, lst):
    base = scal[3]

    def scan(i, n):
        pos = n - base
        valid = meta[3 * i]

        @pl.when((valid == 1) & (pos >= 0) & (pos < ROUND))
        def _():
            lst[pos] = meta[3 * i + 1]
            lst[ROUND + pos] = meta[3 * i + 2]
            lst[2 * ROUND + pos] = i

        return n + valid

    total = lax.fori_loop(0, GROUPS * SLOTS, scan, 0)
    lst[3 * ROUND] = jnp.clip(total - base, 0, ROUND)


def each_tile(own, n, d, work):
    to = jnp.bitwise_and(own + d, NO - 1)

    @pl.loop(0, jnp.right_shift(n - to + NO - 1, 2))
    def _(j):
        work(j, NO * j + to)


def slot_row(slot):
    return (slot // SLOTS) * ROWS + 3 * (slot % SLOTS)


def src_pack_kernel(scal, lst, a00, a10, a30, a2t0, a2b0, a01, a11, a31, a2t1, a2b1, *outs):
    own, x_at, c_at = scal[0], scal[1], scal[2]
    sources = (
        ((a00,), (a01,)), ((a10,), (a11,)), ((a2t0, a2b0), (a2t1, a2b1)), ((a30,), (a31,)),
    )
    for d in range(NO):

        def work(j, k):
            src_at = lst[k]
            cols = lane_block(jnp.bitwise_and(src_at, STORED - 1))
            dx = jnp.bitwise_and(jnp.right_shift(src_at, 5) - x_at, NX - 1)
            dc = jnp.bitwise_and(jnp.right_shift(src_at, 4) + c_at, NC - 1)
            for sx in range(NX):
                for sc in range(NC):

                    @pl.when((dx == sx) & (dc == sc))
                    def _():
                        refs = sources[sx][sc]
                        step = RK // len(refs)
                        for h, ref in enumerate(refs):
                            outs[d][j, h * step : (h + 1) * step, :] = ref[:, cols]

        each_tile(own, lst[3 * ROUND], d, work)


def dst_pack_kernel(scal, lst, recv, b, *rest):
    outs = rest[-NO:]
    for d in range(NO):

        def work(j, k):
            dst_at = lst[ROUND + k]
            row = slot_row(lst[2 * ROUND + k])
            c = as_column(recv[pl.ds(row + 2, 1), :RK])
            cols = lane_block(jnp.bitwise_and(dst_at, STORED - 1))
            outs[d][j, :RK, :] = b[jnp.right_shift(dst_at, 7), :, cols] * c
            for i in range(2):
                outs[d][j, RK + i : RK + i + 1, :] = recv[pl.ds(row + i, 1), :]

        each_tile(scal[0], lst[3 * ROUND], d, work)


def tile_kernel(scal, lst, a0, a1, a2, a3, b0, b1, b2, b3, u0, u1, u2, u3, g0, g1, g2, g3, res):
    own = scal[0]
    n = lst[3 * ROUND]
    a_in, b_in, u_out, g_out = (a0, a1, a2, a3), (b0, b1, b2, b3), (u0, u1, u2, u3), (g0, g1, g2, g3)
    shift = lax.broadcasted_iota(i32, (32, SIDE), 0) % 16

    @pl.loop(0, jnp.right_shift(n - own + NO - 1, 2))
    def _(j):
        a = split(jnp.concatenate([r[j] for r in a_in], axis=0))
        b = split(jnp.concatenate([r[j, :RK] for r in b_in], axis=0))
        res[...] = dot3(a, b, ((0,), (0,)))
        for d in range(NO):
            rows = pl.ds(pl.multiple_of(jnp.bitwise_and(own - d, NO - 1) * 32, 32), 32)
            words = jnp.concatenate(
                [jnp.broadcast_to(b_in[d][j, RK + i : RK + i + 1, :], (16, SIDE)) for i in range(2)], axis=0
            ).astype(i32)
            entries = (jnp.right_shift(words, shift) & 1).astype(f32)
            res[rows, :] = jax.nn.sigmoid(res[rows, :]) - entries
        r = split(res[...])
        u = dot3(b, r, ((1,), (1,)))
        g = dot3(a, r, ((1,), (0,)))
        for d in range(NO):
            u_out[d][j] = u[RK * d : RK * (d + 1)]
            g_out[d][j] = g[RK * d : RK * (d + 1)]


def dst_sum_kernel(scal, lst, recv, b, g0, g1, g2, g3, out, hour):
    out[...] = jnp.zeros_like(out)
    hour[...] = jnp.zeros_like(hour)
    ones = jnp.ones((8, SIDE), f32)
    for d, g in enumerate((g0, g1, g2, g3)):

        def work(j, k):
            dst_at = lst[ROUND + k]
            slot = lst[2 * ROUND + k]
            c = as_column(recv[pl.ds(slot_row(slot) + 2, 1), :RK])
            z = jnp.right_shift(dst_at, 7)
            cols = lane_block(jnp.bitwise_and(dst_at, STORED - 1))
            part = g[j]
            out[z, :, cols] += part * c
            row = lax.dot_general(
                ones, b[z, :, cols] * part, (((1,), (1,)), ((), ())),
                precision=lax.Precision.HIGHEST, preferred_element_type=f32,
            )
            hour[slot // SLOTS, pl.ds(slot % SLOTS, 1), :RK] = row[:1]

        each_tile(scal[0], lst[3 * ROUND], d, work)


def src_sum_kernel(scal, lst, u0, u1, u2, u3, back, keep, give):
    own, x_at, c_at = scal[0], scal[1], scal[2]
    keep[...] = jnp.zeros_like(keep)
    give[...] = jnp.zeros_like(give)
    for d, u in enumerate((u0, u1, u2, u3)):

        def work(j, k):
            src_at = lst[k]
            cols = lane_block(jnp.bitwise_and(src_at, STORED - 1))
            dx = jnp.bitwise_and(jnp.right_shift(src_at, 5) - x_at, NX - 1)
            dc = jnp.bitwise_and(jnp.right_shift(src_at, 4) + c_at, NC - 1)
            for sc, total in enumerate((keep, give)):

                @pl.when(dc == sc)
                def _():
                    total[dx, :, cols] += u[j]

        each_tile(own, lst[3 * ROUND], d, work)


def hour_kernel(scal, hours, where, back, out):
    first_hour = scal[1]
    out[...] = jnp.zeros_like(out)

    @pl.loop(0, TILE_CAP)
    def _(t):
        at = where[t]

        @pl.when(at >= 0)
        def _():
            h = hours[t] - first_hour
            out[pl.ds(h, 1), :] += back[at // 8, pl.ds(at % 8, 1), :RK]


def shape(*dims, dtype=f32):
    return jax.ShapeDtypeStruct(dims, dtype)


def call(kernel, out_shape, in_specs, args, out_specs=None, scratch=()):
    if out_specs is None:
        out_specs = jax.tree.map(lambda _: VMEM, out_shape)
    return pl.pallas_call(
        kernel, out_shape=out_shape, in_specs=in_specs, out_specs=out_specs,
        scratch_shapes=scratch, compiler_params=PARAMS,
    )(*args)


def hop(value, axis, size, by):
    return lax.ppermute(value, axis, [(i, (i + by) % size) for i in range(size)])


def per_device(
    src_factor, dst_factor, hour_factor, tile_src, tile_dst, tile_hour, tile_count, src_place, dst_place, tile_bits
):
    z_at, x_at, c_at, own = (lax.axis_index(n).astype(i32) for n in ("z", "x", "c", "own"))
    first_hour = ((z_at * NX + x_at) * NC + c_at) * hour_factor.shape[0]
    live = tile_count[0]
    half = RK // 2

    with jax.named_scope("gather_dst"):
        b_all = lax.all_gather(dst_factor, "z", axis=0)
    with jax.named_scope("gather_src"):
        up = hop(src_factor, "x", NX, 1)
        down = hop(src_factor, "x", NX, -1)
        far_top = hop(up[:half], "x", NX, 1)
        far_bottom = hop(down[half:], "x", NX, -1)
        mine = (src_factor, down, up, far_top, far_bottom)
        a_all = mine + tuple(hop(v, "c", NC, 1) for v in mine)

    def one_round(pair_round, base):
        with jax.named_scope("slots"):
            scal = jnp.stack([own, first_hour, live, pair_round])
            sent, where = call(
                send_kernel, (shape(GROUPS, ROWS, SIDE), shape(TILE_CAP, dtype=i32)),
                [SMEM] * 6 + [VMEM] * 2,
                (scal, tile_src, tile_dst, tile_hour, src_place, dst_place, tile_bits, hour_factor),
                out_specs=(VMEM, SMEM), scratch=[pltpu.SMEM((GROUPS,), i32)],
            )
            got = lax.all_to_all(sent, SLAB, 0, 0)
            meta = got[:, 2 : ROWS - 1 : 3, RK : RK + 3].astype(i32).reshape(-1)
            rows = got.reshape(GROUPS * ROWS, SIDE)
            hist = got[:, ROWS - 1, :GROUPS].astype(i32)
        at = jnp.stack([own, x_at, c_at, base])
        with jax.named_scope("list"):
            lst = call(list_kernel, shape(3 * ROUND + 8, dtype=i32), [SMEM] * 2, (at, meta), out_specs=SMEM)
        with jax.named_scope("src_exchange"):
            a_out = call(
                src_pack_kernel, (shape(PER, RK, SIDE),) * NO, [SMEM] * 2 + [VMEM] * 10, (at, lst) + a_all
            )
            a_in = [v if d == 0 else hop(v, "own", NO, d) for d, v in enumerate(a_out)]
        with jax.named_scope("dst_exchange"):
            b_out = call(
                dst_pack_kernel, (shape(PER, RK + 8, SIDE),) * NO, [SMEM] * 2 + [VMEM] * 2 + [ANY] * NO,
                (at, lst, rows, b_all, *a_in),
            )
            b_in = [v if d == 0 else hop(v, "own", NO, d) for d, v in enumerate(b_out)]
        with jax.named_scope("tiles"):
            parts = call(
                tile_kernel, (shape(PER, RK, SIDE),) * (2 * NO), [SMEM] * 2 + [VMEM] * 8,
                (at, lst, *a_in, *b_in), scratch=[pltpu.VMEM((SIDE, SIDE), f32)],
            )
        with jax.named_scope("dst_back"):
            g = [v if d == 0 else hop(v, "own", NO, -d) for d, v in enumerate(parts[NO:])]
            g_sum, hour_terms = call(
                dst_sum_kernel, (shape(NZ, RK, STORED * SIDE), shape(GROUPS, 8, SIDE)),
                [SMEM] * 2 + [VMEM] * (2 + NO), (at, lst, rows, b_all, *g),
            )
            grad_dst = lax.psum_scatter(g_sum, "z", scatter_dimension=0)
        with jax.named_scope("hours"):
            back = lax.all_to_all(hour_terms, SLAB, 0, 0)
            grad_hour = call(
                hour_kernel, shape(*hour_factor.shape), [SMEM] * 3 + [VMEM], (scal, tile_hour, where, back)
            )
        with jax.named_scope("src_back"):
            u = [v if d == 0 else hop(v, "own", NO, -d) for d, v in enumerate(parts[:NO])]
            keep, give = call(
                src_sum_kernel, (shape(NX, RK, STORED * SIDE),) * 2, [SMEM] * 2 + [VMEM] * NO + [ANY],
                (at, lst, *u, back),
            )
            s = keep + hop(give, "c", NC, 1)
            top = hop(s[2, :half], "x", NX, 1)
            bottom = hop(s[2, half:], "x", NX, -1)
            one = hop(jnp.concatenate([s[1, :half] + top, s[1, half:]]), "x", NX, 1)
            three = hop(jnp.concatenate([s[3, :half], s[3, half:] + bottom]), "x", NX, -1)
            grad_src = s[0] + one + three
        return (grad_src, grad_dst, grad_hour), hist

    zero = jnp.zeros((), i32)
    grads, hist = one_round(zero, zero)

    def busiest(pair_round):
        return jnp.max(jnp.sum(jnp.clip(hist - pair_round * SLOTS, 0, SLOTS), axis=0))

    def following(pair_round, base):
        more = base + ROUND < busiest(pair_round)
        return jnp.where(more, pair_round, pair_round + 1), jnp.where(more, base + ROUND, 0)

    def body(state):
        pair_round, base, sums = state
        terms, _ = one_round(pair_round, base)
        return following(pair_round, base) + (jax.tree.map(jnp.add, sums, terms),)

    last = lax.while_loop(lambda state: jnp.max(hist) > state[0] * SLOTS, body, following(zero, zero) + (grads,))
    return last[2]


def solution(mesh):
    fine = Mesh(mesh.devices.reshape(NZ, NX, NC, NO), SLAB + ("own",))
    return jax.shard_map(
        per_device,
        mesh=fine,
        in_specs=(
            P("own", SLAB), P("own", SLAB), P(SLAB, "own"), P(SLAB), P(SLAB), P(SLAB), P(SLAB), P(), P(),
            P(SLAB, None, None),
        ),
        out_specs=(P("own", SLAB), P("own", SLAB), P(SLAB, "own")),
        check_vma=False,
    )
```

```python
import jax
import jax.numpy as jnp
from jax import lax
from jax.experimental import pallas as pl
from jax.experimental.pallas import tpu as pltpu
from jax.sharding import Mesh, PartitionSpec as P

NZ, NX, NC, NO = 8, 4, 2, 4
SLAB = ("z", "x", "c")
GROUPS = 64
TILE_CAP = 30
SIDE = 128
RK = 64
RANK = RK * NO
STORED = 16
PART = STORED // NO * SIDE
SLOTS = 5
ROWS = 3 * SLOTS + 1
PER = 16
LIST = NO * PER
XROWS = RK + 8
VMEM = pl.BlockSpec(memory_space=pltpu.VMEM)
SMEM = pl.BlockSpec(memory_space=pltpu.SMEM)
f32, bf16, i32 = jnp.float32, jnp.bfloat16, jnp.int32
PARAMS = pltpu.CompilerParams(vmem_limit_bytes=48 * 1024 * 1024)


def lane_block(within):
    return pl.ds(pl.multiple_of(within * SIDE, SIDE), SIDE)


def split(x):
    hi = x.astype(bf16)
    return hi, (x - hi.astype(f32)).astype(bf16)


def dot3(a, b, dims):
    dg = lambda p, q: lax.dot_general(p, q, (dims, ((), ())), preferred_element_type=f32)
    return dg(a[0], b[0]) + (dg(a[0], b[1]) + dg(a[1], b[0]))


def as_column(row):
    return jnp.broadcast_to(row, (SIDE, RK)).T


def send_kernel(scal, src_ids, dst_ids, hours, src_place, dst_place, bits, hour_rows, out, where, count):
    own, first_hour, live, pair_round = scal[0], scal[1], scal[2], scal[3]

    @pl.loop(0, GROUPS)
    def _(g):
        count[g] = 0

    out[...] = jnp.zeros_like(out)
    lane = lax.broadcasted_iota(i32, (1, SIDE), 1)

    def step(t, told):
        src_at = src_place[src_ids[t]]
        dst_at = dst_place[dst_ids[t]]
        to = jnp.right_shift(src_at, 7) * 8 + jnp.bitwise_and(jnp.right_shift(dst_at, 4), 7)
        rank = count[to]
        slot = rank - pair_round * SLOTS
        here = (t < live) & (slot >= 0) & (slot < SLOTS)
        where[t] = jnp.where(here, to * 8 + slot, -1)

        @pl.when(t < live)
        def _():
            count[to] = rank + 1

        @pl.when(here)
        def _():
            for i in range(2):
                out[to, pl.ds(3 * slot + i, 1), :] = bits[t, pl.ds(2 * own + i, 1), :].astype(f32)
            c = hour_rows[pl.ds(hours[t] - first_hour, 1), :]
            row = jnp.concatenate([c, jnp.zeros_like(c)], axis=1)
            row = jnp.where(lane == 64, 1.0, row)
            row = jnp.where(lane == 65, src_at.astype(f32), row)
            row = jnp.where(lane == 66, dst_at.astype(f32), row)
            out[to, pl.ds(3 * slot + 2, 1), :] = row

        alive = t < live
        told = jnp.where(lane == t, jnp.where(alive, src_at, -1).astype(f32), told)
        told = jnp.where(lane == t + 32, dst_at.astype(f32), told)
        return jnp.where(lane == t + 64, rank.astype(f32), told)

    told = lax.fori_loop(0, TILE_CAP, step, jnp.zeros((1, SIDE), f32))
    out[:, ROWS - 1 : ROWS, :] = jnp.broadcast_to(told[None], (GROUPS, 1, SIDE))


def list_kernel(scal, meta, lst, seen):
    base = scal[3]
    for o in range(NO):
        seen[o] = 0

    @pl.loop(0, GROUPS)
    def _(g):
        for s in range(SLOTS):
            i = g * SLOTS + s

            @pl.when(meta[3 * i] == 1)
            def _():
                dst_at = meta[3 * i + 2]
                to = jnp.bitwise_and(jnp.right_shift(dst_at, 2), NO - 1)
                pos = seen[to] - base
                seen[to] += 1

                @pl.when((pos >= 0) & (pos < PER))
                def _():
                    at = to * PER + pos
                    lst[at] = meta[3 * i + 1]
                    lst[LIST + at] = dst_at
                    lst[2 * LIST + at] = i

    for o in range(NO):
        lst[3 * LIST + o] = jnp.clip(seen[o] - base, 0, PER)


def each_tile(own, lst, d, work):
    to = jnp.bitwise_and(own + d, NO - 1)

    @pl.loop(0, lst[3 * LIST + to])
    def _(j):
        work(j, PER * to + j)


def slot_row(slot):
    return (slot // SLOTS) * ROWS + 3 * (slot % SLOTS)


def src_pack_kernel(scal, lst, recv, a00, a10, a30, a2t0, a2b0, a01, a11, a31, a2t1, a2b1, *outs):
    own, x_at, c_at = scal[0], scal[1], scal[2]
    sources = (
        ((a00,), (a01,)), ((a10,), (a11,)), ((a2t0, a2b0), (a2t1, a2b1)), ((a30,), (a31,)),
    )
    for d in range(NO):

        def work(j, k):
            src_at = lst[k]
            row = slot_row(lst[2 * LIST + k])
            cols = lane_block(jnp.bitwise_and(src_at, STORED - 1))
            dx = jnp.bitwise_and(jnp.right_shift(src_at, 5) - x_at, NX - 1)
            dc = jnp.bitwise_and(jnp.right_shift(src_at, 4) + c_at, NC - 1)
            for sx in range(NX):
                for sc in range(NC):

                    @pl.when((dx == sx) & (dc == sc))
                    def _():
                        refs = sources[sx][sc]
                        step = RK // len(refs)
                        for h, ref in enumerate(refs):
                            outs[d][j, h * step : (h + 1) * step, :] = ref[:, cols]

            for i in range(3):
                outs[d][j, RK + i : RK + i + 1, :] = recv[pl.ds(row + i, 1), :]

        each_tile(own, lst, d, work)


def tile_kernel(scal, lst, a0, a1, a2, a3, b_all, g_sum, u0, u1, u2, u3, res):
    own = scal[0]
    a_in, u_out = (a0, a1, a2, a3), (u0, u1, u2, u3)
    shift = jnp.bitwise_and(lax.broadcasted_iota(i32, (32, SIDE), 0), 15)
    ones = jnp.ones((8, SIDE), f32)
    g_sum[...] = jnp.zeros_like(g_sum)

    def work(j, k):
        dst_at = lst[LIST + k]
        z = jnp.right_shift(dst_at, 7)
        cols = lane_block(jnp.bitwise_and(dst_at, STORED // NO - 1))
        b_raw = b_all[z, :, cols]
        c = jnp.concatenate([as_column(r[j, RK + 2 : RK + 3, :RK]) for r in a_in], axis=0)
        a = split(jnp.concatenate([r[j, :RK] for r in a_in], axis=0))
        b = split(b_raw * c)
        res[...] = dot3(a, b, ((0,), (0,)))
        for d in range(NO):
            rows = pl.ds(pl.multiple_of(jnp.bitwise_and(own - d, NO - 1) * 32, 32), 32)
            words = jnp.concatenate(
                [jnp.broadcast_to(a_in[d][j, RK + i : RK + i + 1, :], (16, SIDE)) for i in range(2)], axis=0
            ).astype(i32)
            entries = jnp.bitwise_and(jnp.right_shift(words, shift), 1).astype(f32)
            res[rows, :] = jax.nn.sigmoid(res[rows, :]) - entries
        r = split(res[...])
        u = dot3(b, r, ((1,), (1,)))
        g = dot3(a, r, ((1,), (0,)))
        g_sum[z, :, cols] += g * c
        h = lax.dot_general(
            ones, b_raw * g, (((1,), (1,)), ((), ())),
            precision=lax.Precision.HIGHEST, preferred_element_type=f32,
        )
        for d in range(NO):
            u_out[d][j, :RK] = u[RK * d : RK * (d + 1)]
            u_out[d][j, RK : RK + 1, :RK] = h[:1, RK * d : RK * (d + 1)]

    each_tile(own, lst, 0, work)


def src_sum_kernel(scal, lst, u0, u1, u2, u3, keep, give, hour):
    own, x_at, c_at = scal[0], scal[1], scal[2]
    for ref in (keep, give, hour):
        ref[...] = jnp.zeros_like(ref)
    for d, u in enumerate((u0, u1, u2, u3)):

        def work(j, k):
            src_at = lst[k]
            slot = lst[2 * LIST + k]
            cols = lane_block(jnp.bitwise_and(src_at, STORED - 1))
            dx = jnp.bitwise_and(jnp.right_shift(src_at, 5) - x_at, NX - 1)
            dc = jnp.bitwise_and(jnp.right_shift(src_at, 4) + c_at, NC - 1)
            for sc, total in enumerate((keep, give)):

                @pl.when(dc == sc)
                def _():
                    total[dx, :, cols] += u[j, :RK]

            hour[slot // SLOTS, pl.ds(slot % SLOTS, 1), :RK] = u[j, RK : RK + 1, :RK]

        each_tile(own, lst, d, work)


def hour_kernel(scal, hours, where, back, out):
    first_hour = scal[1]
    out[...] = jnp.zeros_like(out)

    @pl.loop(0, TILE_CAP)
    def _(t):
        at = where[t]

        @pl.when(at >= 0)
        def _():
            h = hours[t] - first_hour
            out[pl.ds(h, 1), :] += back[jnp.right_shift(at, 3), pl.ds(jnp.bitwise_and(at, 7), 1), :RK]


def shape(*dims, dtype=f32):
    return jax.ShapeDtypeStruct(dims, dtype)


def call(kernel, out_shape, in_specs, args, out_specs=None, scratch=()):
    if out_specs is None:
        out_specs = jax.tree.map(lambda _: VMEM, out_shape)
    return pl.pallas_call(
        kernel, out_shape=out_shape, in_specs=in_specs, out_specs=out_specs,
        scratch_shapes=scratch, compiler_params=PARAMS,
    )(*args)


def hop(value, axis, size, by):
    if by == 0:
        return value
    return lax.ppermute(value, axis, [(i, (i + by) % size) for i in range(size)])


def per_device(
    src_factor, dst_factor, hour_factor, tile_src, tile_dst, tile_hour, tile_count, src_place, dst_place, tile_bits
):
    z_at, x_at, c_at, own = (lax.axis_index(n).astype(i32) for n in ("z", "x", "c", "own"))
    first_hour = ((z_at * NX + x_at) * NC + c_at) * hour_factor.shape[0]
    live = tile_count[0]
    half = RK // 2

    def part_of(d):
        return jnp.bitwise_and(own + d, NO - 1) * PART

    with jax.named_scope("gather_dst"):
        parts = [hop(lax.dynamic_slice(dst_factor, (0, part_of(d)), (RK, PART)), "own", NO, d) for d in range(NO)]
        b_all = lax.all_gather(jnp.concatenate(parts, axis=0), "z", axis=0)
    with jax.named_scope("gather_src"):
        up = hop(src_factor, "x", NX, 1)
        down = hop(src_factor, "x", NX, -1)
        far_top = hop(up[:half], "x", NX, 1)
        far_bottom = hop(down[half:], "x", NX, -1)
        mine = (src_factor, down, up, far_top, far_bottom)
        a_all = mine + tuple(hop(v, "c", NC, 1) for v in mine)

    def one_round(pair_round, base):
        with jax.named_scope("slots"):
            scal = jnp.stack([own, first_hour, live, pair_round])
            sent, where = call(
                send_kernel, (shape(GROUPS, ROWS, SIDE), shape(TILE_CAP, dtype=i32)),
                [SMEM] * 6 + [VMEM] * 2,
                (scal, tile_src, tile_dst, tile_hour, src_place, dst_place, tile_bits, hour_factor),
                out_specs=(VMEM, SMEM), scratch=[pltpu.SMEM((GROUPS,), i32)],
            )
            got = lax.all_to_all(sent, SLAB, 0, 0)
            meta = got[:, 2 : ROWS - 1 : 3, RK : RK + 3].astype(i32).reshape(-1)
            rows = got.reshape(GROUPS * ROWS, SIDE)
            told = got[:, ROWS - 1].astype(i32)
        at = jnp.stack([own, x_at, c_at, base])
        with jax.named_scope("list"):
            lst = call(
                list_kernel, shape(3 * LIST + 8, dtype=i32), [SMEM] * 2, (at, meta), out_specs=SMEM,
                scratch=[pltpu.SMEM((NO,), i32)],
            )
        with jax.named_scope("src_exchange"):
            a_out = call(
                src_pack_kernel, (shape(PER, XROWS, SIDE),) * NO, [SMEM] * 2 + [VMEM] * 11, (at, lst, rows) + a_all
            )
            a_in = [hop(v, "own", NO, d) for d, v in enumerate(a_out)]
        with jax.named_scope("tiles"):
            g_sum, *u_out = call(
                tile_kernel, (shape(NZ, RANK, PART),) + (shape(PER, XROWS, SIDE),) * NO, [SMEM] * 2 + [VMEM] * 5,
                (at, lst, *a_in, b_all), scratch=[pltpu.VMEM((SIDE, SIDE), f32)],
            )
        with jax.named_scope("dst_back"):
            g_part = lax.psum_scatter(g_sum, "z", scatter_dimension=0)
            grad_dst = jnp.zeros_like(dst_factor)
            for d in range(NO):
                piece = hop(g_part[RK * d : RK * (d + 1)], "own", NO, -d)
                grad_dst = lax.dynamic_update_slice(grad_dst, piece, (0, part_of(d)))
        with jax.named_scope("src_back"):
            u = [hop(v, "own", NO, -d) for d, v in enumerate(u_out)]
            keep, give, hour_terms = call(
                src_sum_kernel, (shape(NX, RK, STORED * SIDE),) * 2 + (shape(GROUPS, 8, SIDE),),
                [SMEM] * 2 + [VMEM] * NO, (at, lst, *u),
            )
            s = keep + hop(give, "c", NC, 1)
            top = hop(s[2, :half], "x", NX, 1)
            bottom = hop(s[2, half:], "x", NX, -1)
            one = hop(jnp.concatenate([s[1, :half] + top, s[1, half:]]), "x", NX, 1)
            three = hop(jnp.concatenate([s[3, :half], s[3, half:] + bottom]), "x", NX, -1)
            grad_src = s[0] + one + three
        with jax.named_scope("hours"):
            back = lax.all_to_all(hour_terms, SLAB, 0, 0)
            grad_hour = call(
                hour_kernel, shape(*hour_factor.shape), [SMEM] * 3 + [VMEM], (scal, tile_hour, where, back)
            )
        return (grad_src, grad_dst, grad_hour), told

    zero = jnp.zeros((), i32)
    grads, told = one_round(zero, zero)

    src_at, dst_at, rank = (told[:, 32 * i : 32 * i + TILE_CAP].reshape(-1) for i in range(3))
    worker = (src_at // 128) * 32 + (dst_at // STORED) % 8 * NO + dst_at % STORED // NO
    alive = src_at >= 0

    def busiest(pair_round):
        here = alive & (rank // SLOTS == pair_round)
        counts = jnp.sum((worker[None, :] == jnp.arange(GROUPS * NO, dtype=i32)[:, None]) & here[None, :], axis=1)
        return jnp.max(counts.astype(i32))

    def following(pair_round, base):
        more = base + PER < busiest(pair_round)
        return jnp.where(more, pair_round, pair_round + 1), jnp.where(more, base + PER, 0)

    def body(state):
        pair_round, base, sums = state
        terms, _ = one_round(pair_round, base)
        return following(pair_round, base) + (jax.tree.map(jnp.add, sums, terms),)

    top_rank = jnp.max(jnp.where(alive, rank, -1))
    last = lax.while_loop(lambda state: top_rank >= state[0] * SLOTS, body, following(zero, zero) + (grads,))
    return last[2]


def solution(mesh):
    fine = Mesh(mesh.devices.reshape(NZ, NX, NC, NO), SLAB + ("own",))
    return jax.shard_map(
        per_device,
        mesh=fine,
        in_specs=(
            P("own", SLAB), P("own", SLAB), P(SLAB, "own"), P(SLAB), P(SLAB), P(SLAB), P(SLAB), P(), P(),
            P(SLAB, None, None),
        ),
        out_specs=(P("own", SLAB), P("own", SLAB), P(SLAB, "own")),
        check_vma=False,
    )
```

```python
import jax
import jax.numpy as jnp
from jax import lax
from jax.experimental import pallas as pl
from jax.experimental.pallas import tpu as pltpu
from jax.sharding import Mesh, PartitionSpec as P

NZ, NX, NC, NO = 8, 4, 2, 4
SLAB = ("z", "x", "c")
GROUPS = 64
TILE_CAP = 30
SIDE = 128
RK = 64
RANK = RK * NO
STORED = 16
PART = STORED // NO * SIDE
SLOTS = 5
ROWS = 3 * SLOTS + 1
PER = 16
LIST = NO * PER
XROWS = RK + 8
VMEM = pl.BlockSpec(memory_space=pltpu.VMEM)
SMEM = pl.BlockSpec(memory_space=pltpu.SMEM)
ANY = pl.BlockSpec(memory_space=pl.ANY)
f32, bf16, i32 = jnp.float32, jnp.bfloat16, jnp.int32
PARAMS = pltpu.CompilerParams(vmem_limit_bytes=24 * 1024 * 1024)


def lane_block(within):
    return pl.ds(pl.multiple_of(within * SIDE, SIDE), SIDE)


def split(x):
    hi = x.astype(bf16)
    return hi, (x - hi.astype(f32)).astype(bf16)


def dot3(a, b, dims):
    dg = lambda p, q: lax.dot_general(p, q, (dims, ((), ())), preferred_element_type=f32)
    return dg(a[0], b[0]) + (dg(a[0], b[1]) + dg(a[1], b[0]))


def as_column(row):
    return jnp.broadcast_to(row, (SIDE, RK)).T


def send_kernel(scal, src_ids, dst_ids, hours, src_place, dst_place, bits, hour_rows, out, where, count):
    own, first_hour, live, pair_round = scal[0], scal[1], scal[2], scal[3]

    @pl.loop(0, GROUPS)
    def _(g):
        count[g] = 0

    out[...] = jnp.zeros_like(out)
    lane = lax.broadcasted_iota(i32, (1, SIDE), 1)

    def step(t, told):
        src_at = src_place[src_ids[t]]
        dst_at = dst_place[dst_ids[t]]
        to = jnp.right_shift(src_at, 7) * 8 + jnp.bitwise_and(jnp.right_shift(dst_at, 4), 7)
        rank = count[to]
        slot = rank - pair_round * SLOTS
        here = (t < live) & (slot >= 0) & (slot < SLOTS)
        where[t] = jnp.where(here, to * 8 + slot, -1)

        @pl.when(t < live)
        def _():
            count[to] = rank + 1

        @pl.when(here)
        def _():
            for i in range(2):
                out[to, pl.ds(3 * slot + i, 1), :] = bits[t, pl.ds(2 * own + i, 1), :].astype(f32)
            out[to, pl.ds(3 * slot + 2, 1), :RK] = hour_rows[pl.ds(hours[t] - first_hour, 1), :]
            row = out[to, ROWS - 1 : ROWS, :]
            row = jnp.where(lane == slot, src_at.astype(f32), row)
            row = jnp.where(lane == 8 + slot, dst_at.astype(f32), row)
            out[to, ROWS - 1 : ROWS, :] = jnp.where(lane == 16, (slot + 1).astype(f32), row)

        alive = t < live
        told = jnp.where(lane == t + 32, jnp.where(alive, src_at, -1).astype(f32), told)
        told = jnp.where(lane == t + 64, dst_at.astype(f32), told)
        return jnp.where(lane == t + 96, rank.astype(f32), told)

    told = lax.fori_loop(0, TILE_CAP, step, jnp.zeros((1, SIDE), f32))
    out[:, ROWS - 1 : ROWS, :] += jnp.broadcast_to(told[None], (GROUPS, 1, SIDE))


def list_kernel(scal, got, lst, seen, staged, meta, sem):
    base = scal[3]
    for o in range(NO):
        seen[o] = 0
    staged[...] = got[:, ROWS - 1, :].astype(i32)
    copy = pltpu.make_async_copy(staged, meta, sem)
    copy.start()
    copy.wait()

    @pl.loop(0, GROUPS)
    def _(g):
        n = meta[g, 16]
        for s in range(SLOTS):

            @pl.when(s < n)
            def _():
                dst_at = meta[g, 8 + s]
                to = jnp.bitwise_and(jnp.right_shift(dst_at, 2), NO - 1)
                pos = seen[to] - base
                seen[to] += 1

                @pl.when((pos >= 0) & (pos < PER))
                def _():
                    at = to * PER + pos
                    lst[at] = meta[g, s]
                    lst[LIST + at] = dst_at
                    lst[2 * LIST + at] = g * 8 + s

    for o in range(NO):
        lst[3 * LIST + o] = jnp.clip(seen[o] - base, 0, PER)


def each_tile(own, lst, d, work):
    to = jnp.bitwise_and(own + d, NO - 1)

    @pl.loop(0, lst[3 * LIST + to])
    def _(j):
        work(j, PER * to + j)


def slot_row(slot):
    return jnp.right_shift(slot, 3) * ROWS + 3 * jnp.bitwise_and(slot, 7)


def src_pack_kernel(scal, lst, recv, a00, a10, a30, a2t0, a2b0, a01, a11, a31, a2t1, a2b1, *outs):
    own, x_at, c_at = scal[0], scal[1], scal[2]
    sources = (
        ((a00,), (a01,)), ((a10,), (a11,)), ((a2t0, a2b0), (a2t1, a2b1)), ((a30,), (a31,)),
    )
    for d in range(NO):

        def work(j, k):
            src_at = lst[k]
            row = slot_row(lst[2 * LIST + k])
            cols = lane_block(jnp.bitwise_and(src_at, STORED - 1))
            dx = jnp.bitwise_and(jnp.right_shift(src_at, 5) - x_at, NX - 1)
            dc = jnp.bitwise_and(jnp.right_shift(src_at, 4) + c_at, NC - 1)
            for sx in range(NX):
                for sc in range(NC):

                    @pl.when((dx == sx) & (dc == sc))
                    def _():
                        refs = sources[sx][sc]
                        step = RK // len(refs)
                        for h, ref in enumerate(refs):
                            outs[d][j, h * step : (h + 1) * step, :] = ref[:, cols]

            for i in range(3):
                outs[d][j, RK + i : RK + i + 1, :] = recv[pl.ds(row + i, 1), :]

        each_tile(own, lst, d, work)


def prepare_kernel(scal, lst, a0, a1, a2, a3, high, low, column, entries):
    own = scal[0]
    a_in = (a0, a1, a2, a3)
    shift = jnp.bitwise_and(lax.broadcasted_iota(i32, (32, SIDE), 0), 15)

    def work(j, k):
        high[j], low[j] = split(jnp.concatenate([r[j, :RK] for r in a_in], axis=0))
        column[j] = jnp.concatenate([as_column(r[j, RK + 2 : RK + 3, :RK]) for r in a_in], axis=0)
        for d in range(NO):
            rows = pl.ds(pl.multiple_of(jnp.bitwise_and(own - d, NO - 1) * 32, 32), 32)
            words = jnp.concatenate(
                [jnp.broadcast_to(a_in[d][j, RK + i : RK + i + 1, :], (16, SIDE)) for i in range(2)], axis=0
            ).astype(i32)
            entries[j, rows, :] = jnp.bitwise_and(jnp.right_shift(words, shift), 1).astype(f32)

    each_tile(own, lst, 0, work)


def tile_kernel(scal, lst, high, low, column, entries, b_all, g_sum, u0, u1, u2, u3, h0, h1, h2, h3):
    ones = jnp.ones((8, SIDE), bf16)
    g_sum[...] = jnp.zeros_like(g_sum)

    def work(j, k):
        dst_at = lst[LIST + k]
        z = jnp.right_shift(dst_at, 7)
        cols = lane_block(jnp.bitwise_and(dst_at, STORED // NO - 1))
        b_raw = b_all[z, :, cols]
        c = column[j]
        a = high[j], low[j]
        b = split(b_raw * c)
        r = split(jax.nn.sigmoid(dot3(a, b, ((0,), (0,)))) - entries[j])
        u = dot3(b, r, ((1,), (1,)))
        g = dot3(a, r, ((1,), (0,)))
        g_sum[z, :, cols] += g * c
        along = lambda x: lax.dot_general(ones, x, (((1,), (1,)), ((), ())), preferred_element_type=f32)
        h_high, h_low = split(b_raw * g)
        h = along(h_high) + along(h_low)
        for d, (u_out, h_out) in enumerate(zip((u0, u1, u2, u3), (h0, h1, h2, h3))):
            u_out[j] = u[RK * d : RK * (d + 1)]
            h_out[pl.ds(j, 1), :RK] = h[:1, RK * d : RK * (d + 1)]

    each_tile(scal[0], lst, 0, work)


def hour_pack_kernel(scal, lst, h0, h1, h2, h3, hour):
    hour[...] = jnp.zeros_like(hour)
    for d, h in enumerate((h0, h1, h2, h3)):

        def work(j, k):
            slot = lst[2 * LIST + k]
            hour[jnp.right_shift(slot, 3), pl.ds(jnp.bitwise_and(slot, 7), 1), :RK] = h[pl.ds(j, 1), :RK]

        each_tile(scal[0], lst, d, work)


def src_sum_kernel(scal, lst, u0, u1, u2, u3, back, keep, give):
    own, x_at, c_at = scal[0], scal[1], scal[2]
    keep[...] = jnp.zeros_like(keep)
    give[...] = jnp.zeros_like(give)
    for d, u in enumerate((u0, u1, u2, u3)):

        def work(j, k):
            src_at = lst[k]
            cols = lane_block(jnp.bitwise_and(src_at, STORED - 1))
            dx = jnp.bitwise_and(jnp.right_shift(src_at, 5) - x_at, NX - 1)
            dc = jnp.bitwise_and(jnp.right_shift(src_at, 4) + c_at, NC - 1)
            for sc, total in enumerate((keep, give)):

                @pl.when(dc == sc)
                def _():
                    total[dx, :, cols] += u[j]

        each_tile(own, lst, d, work)


def stack_kernel(p0, p1, p2, p3, out):
    for d, p in enumerate((p0, p1, p2, p3)):
        out[RK * d : RK * (d + 1), :] = p[...]


def join_kernel(scal, p0, p1, p2, p3, out):
    for d, p in enumerate((p0, p1, p2, p3)):
        to = jnp.bitwise_and(scal[0] + d, NO - 1)
        out[:, pl.ds(pl.multiple_of(to * PART, PART), PART)] = p[...]


def hour_kernel(scal, hours, where, back, out):
    first_hour = scal[1]
    out[...] = jnp.zeros_like(out)

    @pl.loop(0, TILE_CAP)
    def _(t):
        at = where[t]

        @pl.when(at >= 0)
        def _():
            h = hours[t] - first_hour
            out[pl.ds(h, 1), :] += back[jnp.right_shift(at, 3), pl.ds(jnp.bitwise_and(at, 7), 1), :RK]


def shape(*dims, dtype=f32):
    return jax.ShapeDtypeStruct(dims, dtype)


def call(kernel, out_shape, in_specs, args, out_specs=None, scratch=()):
    if out_specs is None:
        out_specs = jax.tree.map(lambda _: VMEM, out_shape)
    return pl.pallas_call(
        kernel, out_shape=out_shape, in_specs=in_specs, out_specs=out_specs,
        scratch_shapes=scratch, compiler_params=PARAMS,
    )(*args)


def hop(value, axis, size, by):
    if by == 0:
        return value
    return lax.ppermute(value, axis, [(i, (i + by) % size) for i in range(size)])


def per_device(
    src_factor, dst_factor, hour_factor, tile_src, tile_dst, tile_hour, tile_count, src_place, dst_place, tile_bits
):
    z_at, x_at, c_at, own = (lax.axis_index(n).astype(i32) for n in ("z", "x", "c", "own"))
    first_hour = ((z_at * NX + x_at) * NC + c_at) * hour_factor.shape[0]
    live = tile_count[0]
    half = RK // 2

    def part_of(d):
        return jnp.bitwise_and(own + d, NO - 1) * PART

    def one_round(pair_round, base, src_factor, dst_factor):
        src_factor, dst_factor, pair_round = lax.optimization_barrier((src_factor, dst_factor, pair_round))
        with jax.named_scope("slots"):
            scal = jnp.stack([own, first_hour, live, pair_round])
            sent, where = call(
                send_kernel, (shape(GROUPS, ROWS, SIDE), shape(TILE_CAP, dtype=i32)),
                [SMEM] * 6 + [VMEM] * 2,
                (scal, tile_src, tile_dst, tile_hour, src_place, dst_place, tile_bits, hour_factor),
                out_specs=(VMEM, SMEM), scratch=[pltpu.SMEM((GROUPS,), i32)],
            )
        with jax.named_scope("gather_dst"):
            parts = [
                hop(lax.dynamic_slice(dst_factor, (0, part_of(d)), (RK, PART)), "own", NO, d) for d in range(NO)
            ]
            parts, sent = lax.optimization_barrier((parts, sent))
            b_mine = call(stack_kernel, shape(RANK, PART), [VMEM] * NO, parts)
            b_all = lax.all_gather(b_mine, "z", axis=0)
        with jax.named_scope("slots"):
            got = lax.all_to_all(sent, SLAB, 0, 0)
            rows = got.reshape(GROUPS * ROWS, SIDE)
            told = got[:, ROWS - 1].astype(i32)
        with jax.named_scope("gather_src"):
            stored, _ = lax.optimization_barrier((src_factor, b_mine))
            up = hop(stored, "x", NX, 1)
            down = hop(stored, "x", NX, -1)
            far_top = hop(up[:half], "x", NX, 1)
            far_bottom = hop(down[half:], "x", NX, -1)
            mine = (stored, down, up, far_top, far_bottom)
            a_all = mine + tuple(hop(v, "c", NC, 1) for v in mine)
        at = jnp.stack([own, x_at, c_at, base])
        with jax.named_scope("list"):
            lst = call(
                list_kernel, shape(3 * LIST + 8, dtype=i32), [SMEM, VMEM], (at, got), out_specs=SMEM,
                scratch=[
                    pltpu.SMEM((NO,), i32), pltpu.VMEM((GROUPS, SIDE), i32), pltpu.SMEM((GROUPS, SIDE), i32),
                    pltpu.SemaphoreType.DMA,
                ],
            )
        with jax.named_scope("src_exchange"):
            a_out = call(
                src_pack_kernel, (shape(PER, XROWS, SIDE),) * NO, [SMEM] * 2 + [VMEM] * 11, (at, lst, rows) + a_all
            )
            a_in = [hop(v, "own", NO, d) for d, v in enumerate(a_out)]
            ready = call(
                prepare_kernel,
                (shape(PER, RANK, SIDE, dtype=bf16),) * 2 + (shape(PER, RANK, SIDE), shape(PER, SIDE, SIDE)),
                [SMEM] * 2 + [VMEM] * NO, (at, lst, *a_in),
            )
        with jax.named_scope("tiles"):
            g_sum, *out = call(
                tile_kernel,
                (shape(NZ, RANK, PART),) + (shape(PER, RK, SIDE),) * NO + (shape(PER, SIDE),) * NO,
                [SMEM] * 2 + [VMEM] * 5, (at, lst, *ready, b_all),
            )
        with jax.named_scope("hours"):
            h = [hop(v, "own", NO, -d) for d, v in enumerate(out[NO:])]
            hour_terms = call(hour_pack_kernel, shape(GROUPS, 8, SIDE), [SMEM] * 2 + [VMEM] * NO, (at, lst, *h))
            back = lax.all_to_all(hour_terms, SLAB, 0, 0)
            grad_hour = call(
                hour_kernel, shape(*hour_factor.shape), [SMEM] * 3 + [VMEM], (scal, tile_hour, where, back)
            )
        with jax.named_scope("src_back"):
            u = [hop(v, "own", NO, -d) for d, v in enumerate(out[:NO])]
            keep, give = call(
                src_sum_kernel, (shape(NX, RK, STORED * SIDE),) * 2, [SMEM] * 2 + [VMEM] * NO + [ANY],
                (at, lst, *u, back),
            )
            s = keep + hop(give, "c", NC, 1)
            top = hop(s[2, :half], "x", NX, 1)
            bottom = hop(s[2, half:], "x", NX, -1)
            one = hop(jnp.concatenate([s[1, :half] + top, s[1, half:]]), "x", NX, 1)
            three = hop(jnp.concatenate([s[3, :half], s[3, half:] + bottom]), "x", NX, -1)
            grad_src = s[0] + one + three
        with jax.named_scope("dst_back"):
            g_part = lax.psum_scatter(g_sum, "z", scatter_dimension=0)
            pieces = [hop(g_part[RK * d : RK * (d + 1)], "own", NO, -d) for d in range(NO)]
            grad_dst = call(join_kernel, shape(*dst_factor.shape), [SMEM] + [VMEM] * NO, (at, *pieces))
        return (grad_src, grad_dst, grad_hour), told

    zero = jnp.zeros((), i32)
    grads, told = one_round(zero, zero, src_factor, dst_factor)

    src_at, dst_at, rank = (told[:, 32 * i : 32 * i + TILE_CAP].reshape(-1) for i in range(1, 4))
    worker = (src_at // 128) * 32 + (dst_at // STORED) % 8 * NO + dst_at % STORED // NO
    alive = src_at >= 0

    def busiest(pair_round):
        here = alive & (rank // SLOTS == pair_round)
        counts = jnp.sum((worker[None, :] == jnp.arange(GROUPS * NO, dtype=i32)[:, None]) & here[None, :], axis=1)
        return jnp.max(counts.astype(i32))

    def following(pair_round, base):
        more = base + PER < busiest(pair_round)
        return jnp.where(more, pair_round, pair_round + 1), jnp.where(more, base + PER, 0)

    def body(state):
        pair_round, base, sums = state
        terms, _ = one_round(pair_round, base, src_factor, dst_factor)
        return following(pair_round, base) + (jax.tree.map(jnp.add, sums, terms),)

    top_rank = jnp.max(jnp.where(alive, rank, -1))
    last = lax.while_loop(lambda state: top_rank >= state[0] * SLOTS, body, following(zero, zero) + (grads,))
    return last[2]


def solution(mesh):
    fine = Mesh(mesh.devices.reshape(NZ, NX, NC, NO), SLAB + ("own",))
    return jax.shard_map(
        per_device,
        mesh=fine,
        in_specs=(
            P("own", SLAB), P("own", SLAB), P(SLAB, "own"), P(SLAB), P(SLAB), P(SLAB), P(SLAB), P(), P(),
            P(SLAB, None, None),
        ),
        out_specs=(P("own", SLAB), P("own", SLAB), P(SLAB, "own")),
        check_vma=False,
    )
```

```python
import jax
import jax.numpy as jnp
from jax import lax
from jax.experimental import pallas as pl
from jax.experimental.pallas import tpu as pltpu
from jax.sharding import Mesh, PartitionSpec as P

NZ, NX, NC, NO = 8, 4, 2, 4
SLAB = ("z", "x", "c")
GROUPS = 64
TILE_CAP = 30
SIDE = 128
RK = 64
RANK = RK * NO
STORED = 16
PART = STORED // NO * SIDE
SLOTS = 5
ROWS = 3 * SLOTS + 1
PER = 16
LIST = NO * PER
XROWS = RK + 8
VMEM = pl.BlockSpec(memory_space=pltpu.VMEM)
SMEM = pl.BlockSpec(memory_space=pltpu.SMEM)
ANY = pl.BlockSpec(memory_space=pl.ANY)
HBM = pl.BlockSpec(memory_space=pltpu.HBM)
f32, bf16, i32 = jnp.float32, jnp.bfloat16, jnp.int32
MIB = 1024 * 1024


def lane_block(within):
    return pl.ds(pl.multiple_of(within * SIDE, SIDE), SIDE)


def split(x):
    hi = x.astype(bf16)
    return hi, (x - hi.astype(f32)).astype(bf16)


def dot3(a, b, dims):
    dg = lambda p, q: lax.dot_general(p, q, (dims, ((), ())), preferred_element_type=f32)
    return dg(a[0], b[0]) + (dg(a[0], b[1]) + dg(a[1], b[0]))


def as_column(row):
    return jnp.broadcast_to(row, (SIDE, RK)).T


def send_kernel(scal, src_ids, dst_ids, hours, src_place, dst_place, bits, hour_rows, out, where, count):
    own, first_hour, live, pair_round = scal[0], scal[1], scal[2], scal[3]

    @pl.loop(0, GROUPS)
    def _(g):
        count[g] = 0

    out[...] = jnp.zeros_like(out)
    lane = lax.broadcasted_iota(i32, (1, SIDE), 1)

    def step(t, told):
        src_at = src_place[src_ids[t]]
        dst_at = dst_place[dst_ids[t]]
        to = jnp.right_shift(src_at, 7) * 8 + jnp.bitwise_and(jnp.right_shift(dst_at, 4), 7)
        rank = count[to]
        slot = rank - pair_round * SLOTS
        here = (t < live) & (slot >= 0) & (slot < SLOTS)
        where[t] = jnp.where(here, to * 8 + slot, -1)

        @pl.when(t < live)
        def _():
            count[to] = rank + 1

        @pl.when(here)
        def _():
            for i in range(2):
                out[to, pl.ds(3 * slot + i, 1), :] = bits[t, pl.ds(2 * own + i, 1), :].astype(f32)
            out[to, pl.ds(3 * slot + 2, 1), :RK] = hour_rows[pl.ds(hours[t] - first_hour, 1), :]
            row = out[to, ROWS - 1 : ROWS, :]
            row = jnp.where(lane == slot, src_at.astype(f32), row)
            row = jnp.where(lane == 8 + slot, dst_at.astype(f32), row)
            out[to, ROWS - 1 : ROWS, :] = jnp.where(lane == 16, (slot + 1).astype(f32), row)

        alive = t < live
        told = jnp.where(lane == t + 32, jnp.where(alive, src_at, -1).astype(f32), told)
        told = jnp.where(lane == t + 64, dst_at.astype(f32), told)
        return jnp.where(lane == t + 96, rank.astype(f32), told)

    told = lax.fori_loop(0, TILE_CAP, step, jnp.zeros((1, SIDE), f32))
    out[:, ROWS - 1 : ROWS, :] += jnp.broadcast_to(told[None], (GROUPS, 1, SIDE))


def list_kernel(scal, got, lst, seen, staged, meta, sem):
    base = scal[3]
    for o in range(NO):
        seen[o] = 0
    staged[...] = got[:, ROWS - 1, :].astype(i32)
    copy = pltpu.make_async_copy(staged, meta, sem)
    copy.start()
    copy.wait()

    @pl.loop(0, GROUPS)
    def _(g):
        @pl.loop(0, meta[g, 16])
        def _(i):
            dst_at = meta[g, 8 + i]
            to = jnp.bitwise_and(jnp.right_shift(dst_at, 2), NO - 1)
            pos = seen[to] - base
            seen[to] += 1

            @pl.when((pos >= 0) & (pos < PER))
            def _():
                at = to * PER + pos
                lst[at] = meta[g, i]
                lst[LIST + at] = dst_at
                lst[2 * LIST + at] = g * 8 + i

    for o in range(NO):
        lst[3 * LIST + o] = jnp.clip(seen[o] - base, 0, PER)


def each_tile(own, lst, d, work):
    to = jnp.bitwise_and(own + d, NO - 1)

    @pl.loop(0, lst[3 * LIST + to])
    def _(j):
        work(j, PER * to + j)


def slot_row(slot):
    return jnp.right_shift(slot, 3) * ROWS + 3 * jnp.bitwise_and(slot, 7)


def src_pack_kernel(scal, lst, recv, a00, a10, a30, a2t0, a2b0, a01, a11, a31, a2t1, a2b1, *outs):
    own, x_at, c_at = scal[0], scal[1], scal[2]
    sources = (
        ((a00,), (a01,)), ((a10,), (a11,)), ((a2t0, a2b0), (a2t1, a2b1)), ((a30,), (a31,)),
    )
    for d in range(NO):

        def work(j, k):
            src_at = lst[k]
            row = slot_row(lst[2 * LIST + k])
            cols = lane_block(jnp.bitwise_and(src_at, STORED - 1))
            dx = jnp.bitwise_and(jnp.right_shift(src_at, 5) - x_at, NX - 1)
            dc = jnp.bitwise_and(jnp.right_shift(src_at, 4) + c_at, NC - 1)
            for sx in range(NX):
                for sc in range(NC):

                    @pl.when((dx == sx) & (dc == sc))
                    def _():
                        refs = sources[sx][sc]
                        step = RK // len(refs)
                        for h, ref in enumerate(refs):
                            outs[d][j, h * step : (h + 1) * step, :] = ref[:, cols]

            for i in range(3):
                outs[d][j, RK + i : RK + i + 1, :] = recv[pl.ds(row + i, 1), :]

        each_tile(own, lst, d, work)


def tile_kernel(
    scal, lst, a0, a1, a2, a3, b_all, g_out, u0, u1, u2, u3, h0, h1, h2, h3,
    blocks, g_sum, u_sum, entries, in_sems, out_sems,
):
    own = scal[0]
    a_in, u_out, h_out = (a0, a1, a2, a3), (u0, u1, u2, u3), (h0, h1, h2, h3)
    n = lst[3 * LIST + own]
    shift = jnp.bitwise_and(lax.broadcasted_iota(i32, (32, SIDE), 0), 15)
    ones = jnp.ones((8, SIDE), bf16)

    def place(j):
        dst_at = lst[LIST + PER * own + j]
        return jnp.right_shift(dst_at, 7), lane_block(jnp.bitwise_and(dst_at, STORED // NO - 1))

    def fetch(j):
        z, cols = place(j)
        return pltpu.make_async_copy(b_all.at[z, :, cols], blocks.at[j], in_sems.at[j])

    @pl.loop(0, n)
    def _(j):
        fetch(j).start()

    g_sum[...] = jnp.zeros_like(g_sum)

    @pl.loop(0, n)
    def _(j):
        a = split(jnp.concatenate([r[j, :RK] for r in a_in], axis=0))
        c = jnp.concatenate([as_column(r[j, RK + 2 : RK + 3, :RK]) for r in a_in], axis=0)
        for d in range(NO):
            rows = pl.ds(pl.multiple_of(jnp.bitwise_and(own - d, NO - 1) * 32, 32), 32)
            words = jnp.concatenate(
                [jnp.broadcast_to(a_in[d][j, RK + i : RK + i + 1, :], (16, SIDE)) for i in range(2)], axis=0
            ).astype(i32)
            entries[rows, :] = jnp.bitwise_and(jnp.right_shift(words, shift), 1).astype(f32)
        fetch(j).wait()
        z, cols = place(j)
        b_raw = blocks[j]
        b = split(b_raw * c)
        r = split(jax.nn.sigmoid(dot3(a, b, ((0,), (0,)))) - entries[...])
        u = dot3(b, r, ((1,), (1,)))
        g = dot3(a, r, ((1,), (0,)))
        g_sum[z, :, cols] += g * c
        along = lambda x: lax.dot_general(ones, x, (((1,), (1,)), ((), ())), preferred_element_type=f32)
        h_high, h_low = split(b_raw * g)
        h = along(h_high) + along(h_low)
        for d in range(NO):
            u_sum[d, j] = u[RK * d : RK * (d + 1)]
            h_out[d][pl.ds(j, 1), :RK] = h[:1, RK * d : RK * (d + 1)]

    copies = [pltpu.make_async_copy(g_sum.at[z], g_out.at[z], out_sems.at[z]) for z in range(NZ)]
    copies += [pltpu.make_async_copy(u_sum.at[d], u_out[d], out_sems.at[NZ + d]) for d in range(NO)]
    for copy in copies:
        copy.start()
    for copy in copies:
        copy.wait()


def hour_pack_kernel(scal, lst, h0, h1, h2, h3, hour):
    hour[...] = jnp.zeros_like(hour)
    upper = jnp.right_shift(lax.broadcasted_iota(i32, (1, SIDE), 1), 6)
    for d, h in enumerate((h0, h1, h2, h3)):

        def work(j, k):
            slot = lst[2 * LIST + k]
            g, i = jnp.right_shift(slot, 3), jnp.bitwise_and(slot, 7)
            cols = lane_block(jnp.right_shift(i, 1))
            row = h[pl.ds(j, 1), :RK]
            both = jnp.concatenate([row, row], axis=1)
            hour[g, :, cols] = jnp.where(upper == jnp.bitwise_and(i, 1), both, hour[g, :, cols])

        each_tile(scal[0], lst, d, work)


def src_sum_kernel(scal, lst, u0, u1, u2, u3, hour_terms, keep, give):
    own, x_at, c_at = scal[0], scal[1], scal[2]
    keep[...] = jnp.zeros_like(keep)
    give[...] = jnp.zeros_like(give)
    for d, u in enumerate((u0, u1, u2, u3)):

        def work(j, k):
            src_at = lst[k]
            cols = lane_block(jnp.bitwise_and(src_at, STORED - 1))
            dx = jnp.bitwise_and(jnp.right_shift(src_at, 5) - x_at, NX - 1)
            dc = jnp.bitwise_and(jnp.right_shift(src_at, 4) + c_at, NC - 1)
            for sc, total in enumerate((keep, give)):

                @pl.when(dc == sc)
                def _():
                    total[dx, :, cols] += u[j]

        each_tile(own, lst, d, work)


def stack_kernel(p0, p1, p2, p3, out):
    for d, p in enumerate((p0, p1, p2, p3)):
        out[RK * d : RK * (d + 1), :] = p[...]


def join_kernel(scal, p0, p1, p2, p3, out):
    for d, p in enumerate((p0, p1, p2, p3)):
        to = jnp.bitwise_and(scal[0] + d, NO - 1)
        out[:, pl.ds(pl.multiple_of(to * PART, PART), PART)] = p[...]


def hour_kernel(scal, hours, where, back, out):
    first_hour = scal[1]
    out[...] = jnp.zeros_like(out)

    @pl.loop(0, TILE_CAP)
    def _(t):
        at = where[t]

        @pl.when(at >= 0)
        def _():
            h = hours[t] - first_hour
            slot = jnp.bitwise_and(at, 7)
            both = back[jnp.right_shift(at, 3), :, lane_block(jnp.right_shift(slot, 1))]
            odd = jnp.broadcast_to(jnp.bitwise_and(slot, 1), (1, RK)) == 1
            out[pl.ds(h, 1), :] += jnp.where(odd, both[:, RK:], both[:, :RK])


def shape(*dims, dtype=f32):
    return jax.ShapeDtypeStruct(dims, dtype)


def call(kernel, out_shape, in_specs, args, out_specs=None, scratch=(), vmem=24):
    if out_specs is None:
        out_specs = jax.tree.map(lambda _: VMEM, out_shape)
    return pl.pallas_call(
        kernel, out_shape=out_shape, in_specs=in_specs, out_specs=out_specs,
        scratch_shapes=scratch, compiler_params=pltpu.CompilerParams(vmem_limit_bytes=vmem * MIB),
    )(*args)


def hop(value, axis, size, by):
    if by == 0:
        return value
    return lax.ppermute(value, axis, [(i, (i + by) % size) for i in range(size)])


def per_device(
    src_factor, dst_factor, hour_factor, tile_src, tile_dst, tile_hour, tile_count, src_place, dst_place, tile_bits
):
    z_at, x_at, c_at, own = (lax.axis_index(n).astype(i32) for n in ("z", "x", "c", "own"))
    first_hour = ((z_at * NX + x_at) * NC + c_at) * hour_factor.shape[0]
    live = tile_count[0]
    half = RK // 2

    def part_of(d):
        return jnp.bitwise_and(own + d, NO - 1) * PART

    def one_round(pair_round, base, src_factor, dst_factor):
        src_factor, dst_factor, pair_round = lax.optimization_barrier((src_factor, dst_factor, pair_round))
        with jax.named_scope("slots"):
            scal = jnp.stack([own, first_hour, live, pair_round])
            sent, where = call(
                send_kernel, (shape(GROUPS, ROWS, SIDE), shape(TILE_CAP, dtype=i32)),
                [SMEM] * 6 + [VMEM] * 2,
                (scal, tile_src, tile_dst, tile_hour, src_place, dst_place, tile_bits, hour_factor),
                out_specs=(VMEM, SMEM), scratch=[pltpu.SMEM((GROUPS,), i32)],
            )
        with jax.named_scope("gather_dst"):
            parts = [
                hop(lax.dynamic_slice(dst_factor, (0, part_of(d)), (RK, PART)), "own", NO, d) for d in range(NO)
            ]
            parts, sent = lax.optimization_barrier((parts, sent))
            b_mine = call(stack_kernel, shape(RANK, PART), [VMEM] * NO, parts)
            b_all = lax.all_gather(b_mine, "z", axis=0)
        with jax.named_scope("slots"):
            got = lax.all_to_all(sent, SLAB, 0, 0)
            rows = got.reshape(GROUPS * ROWS, SIDE)
            told = got[:, ROWS - 1].astype(i32)
        with jax.named_scope("gather_src"):
            stored, _ = lax.optimization_barrier((src_factor, b_mine))
            up = hop(stored, "x", NX, 1)
            down = hop(stored, "x", NX, -1)
            far_top = hop(up[:half], "x", NX, 1)
            far_bottom = hop(down[half:], "x", NX, -1)
            mine = (stored, down, up, far_top, far_bottom)
            a_all = mine + tuple(hop(v, "c", NC, 1) for v in mine)
        at = jnp.stack([own, x_at, c_at, base])
        with jax.named_scope("list"):
            lst = call(
                list_kernel, shape(3 * LIST + 8, dtype=i32), [SMEM, VMEM], (at, got), out_specs=SMEM,
                scratch=[
                    pltpu.SMEM((NO,), i32), pltpu.VMEM((GROUPS, SIDE), i32), pltpu.SMEM((GROUPS, SIDE), i32),
                    pltpu.SemaphoreType.DMA,
                ],
            )
        with jax.named_scope("src_exchange"):
            a_out = call(
                src_pack_kernel, (shape(PER, XROWS, SIDE),) * NO, [SMEM] * 2 + [VMEM] * 11, (at, lst, rows) + a_all
            )
            a_in = [hop(v, "own", NO, d) for d, v in enumerate(a_out)]
        with jax.named_scope("tiles"):
            g_sum, *out = call(
                tile_kernel,
                (shape(NZ, RANK, PART),) + (shape(PER, RK, SIDE),) * NO + (shape(PER, SIDE),) * NO,
                [SMEM] * 2 + [VMEM] * NO + [HBM], (at, lst, *a_in, b_all), out_specs=(HBM,) * (1 + NO) + (VMEM,) * NO,
                scratch=[
                    pltpu.VMEM((PER, RANK, SIDE), f32), pltpu.VMEM((NZ, RANK, PART), f32),
                    pltpu.VMEM((NO, PER, RK, SIDE), f32), pltpu.VMEM((SIDE, SIDE), f32),
                    pltpu.SemaphoreType.DMA((PER,)), pltpu.SemaphoreType.DMA((NZ + NO,)),
                ],
                vmem=60,
            )
        with jax.named_scope("hours"):
            h = [hop(v, "own", NO, -d) for d, v in enumerate(out[NO:])]
            hour_terms = call(hour_pack_kernel, shape(GROUPS, 1, 3 * SIDE), [SMEM] * 2 + [VMEM] * NO, (at, lst, *h))
            back = lax.all_to_all(hour_terms, SLAB, 0, 0)
            grad_hour = call(
                hour_kernel, shape(*hour_factor.shape), [SMEM] * 3 + [VMEM], (scal, tile_hour, where, back)
            )
        with jax.named_scope("src_back"):
            u = [hop(v, "own", NO, -d) for d, v in enumerate(out[:NO])]
            keep, give = call(
                src_sum_kernel, (shape(NX, RK, STORED * SIDE),) * 2, [SMEM] * 2 + [VMEM] * NO + [ANY],
                (at, lst, *u, hour_terms),
            )
            s, _ = lax.optimization_barrier((keep + hop(give, "c", NC, 1), back))
            top = hop(s[2, :half], "x", NX, 1)
            bottom = hop(s[2, half:], "x", NX, -1)
            one = hop(jnp.concatenate([s[1, :half] + top, s[1, half:]]), "x", NX, 1)
            three = hop(jnp.concatenate([s[3, :half], s[3, half:] + bottom]), "x", NX, -1)
            grad_src = s[0] + one + three
        with jax.named_scope("dst_back"):
            g_part = lax.psum_scatter(g_sum, "z", scatter_dimension=0)
            pieces = [hop(g_part[RK * d : RK * (d + 1)], "own", NO, -d) for d in range(NO)]
            grad_dst = call(join_kernel, shape(*dst_factor.shape), [SMEM] + [VMEM] * NO, (at, *pieces))
        return (grad_src, grad_dst, grad_hour), told

    zero = jnp.zeros((), i32)
    grads, told = one_round(zero, zero, src_factor, dst_factor)

    src_at, dst_at, rank = (told[:, 32 * i : 32 * i + TILE_CAP].reshape(-1) for i in range(1, 4))
    worker = (src_at // 128) * 32 + (dst_at // STORED) % 8 * NO + dst_at % STORED // NO
    alive = src_at >= 0

    def busiest(pair_round):
        here = alive & (rank // SLOTS == pair_round)
        counts = jnp.sum((worker[None, :] == jnp.arange(GROUPS * NO, dtype=i32)[:, None]) & here[None, :], axis=1)
        return jnp.max(counts.astype(i32))

    def following(pair_round, base):
        more = base + PER < busiest(pair_round)
        return jnp.where(more, pair_round, pair_round + 1), jnp.where(more, base + PER, 0)

    def body(state):
        pair_round, base, sums = state
        terms, _ = one_round(pair_round, base, src_factor, dst_factor)
        return following(pair_round, base) + (jax.tree.map(jnp.add, sums, terms),)

    top_rank = jnp.max(jnp.where(alive, rank, -1))
    last = lax.while_loop(lambda state: top_rank >= state[0] * SLOTS, body, following(zero, zero) + (grads,))
    return last[2]


def solution(mesh):
    fine = Mesh(mesh.devices.reshape(NZ, NX, NC, NO), SLAB + ("own",))
    return jax.shard_map(
        per_device,
        mesh=fine,
        in_specs=(
            P("own", SLAB), P("own", SLAB), P(SLAB, "own"), P(SLAB), P(SLAB), P(SLAB), P(SLAB), P(), P(),
            P(SLAB, None, None),
        ),
        out_specs=(P("own", SLAB), P("own", SLAB), P(SLAB, "own")),
        check_vma=False,
    )
```

```python
import jax
import jax.numpy as jnp
from jax import lax
from jax.experimental import pallas as pl
from jax.experimental.pallas import tpu as pltpu
from jax.sharding import Mesh, PartitionSpec as P

NZ, NX, NC, NO = 8, 4, 2, 4
SLAB = ("z", "x", "c")
GROUPS = 64
TILE_CAP = 30
SIDE = 128
RK = 64
RANK = RK * NO
STORED = 16
PART = STORED // NO * SIDE
SLOTS = 5
ROWS = 3 * SLOTS + 1
PER = 16
LIST = NO * PER
XROWS = RK + 8
VMEM = pl.BlockSpec(memory_space=pltpu.VMEM)
SMEM = pl.BlockSpec(memory_space=pltpu.SMEM)
ANY = pl.BlockSpec(memory_space=pl.ANY)
HBM = pl.BlockSpec(memory_space=pltpu.HBM)
f32, bf16, i32 = jnp.float32, jnp.bfloat16, jnp.int32
MIB = 1024 * 1024


def lane_block(within):
    return pl.ds(pl.multiple_of(within * SIDE, SIDE), SIDE)


def split(x):
    hi = x.astype(bf16)
    return hi, (x - hi.astype(f32)).astype(bf16)


def dot3(a, b, dims):
    dg = lambda p, q: lax.dot_general(p, q, (dims, ((), ())), preferred_element_type=f32)
    return dg(a[0], b[0]) + (dg(a[0], b[1]) + dg(a[1], b[0]))


def as_column(row):
    return jnp.broadcast_to(row, (SIDE, RK)).T


def send_kernel(scal, src_ids, dst_ids, hours, src_place, dst_place, bits, hour_rows, out, where, count):
    own, first_hour, live, pair_round = scal[0], scal[1], scal[2], scal[3]

    @pl.loop(0, GROUPS)
    def _(g):
        count[g] = 0

    out[...] = jnp.zeros_like(out)
    lane = lax.broadcasted_iota(i32, (1, SIDE), 1)

    def step(t, told):
        src_at = src_place[src_ids[t]]
        dst_at = dst_place[dst_ids[t]]
        to = jnp.right_shift(src_at, 7) * 8 + jnp.bitwise_and(jnp.right_shift(dst_at, 4), 7)
        rank = count[to]
        slot = rank - pair_round * SLOTS
        here = (t < live) & (slot >= 0) & (slot < SLOTS)
        where[t] = jnp.where(here, to * 8 + slot, -1)

        @pl.when(t < live)
        def _():
            count[to] = rank + 1

        @pl.when(here)
        def _():
            for i in range(2):
                out[to, pl.ds(3 * slot + i, 1), :] = bits[t, pl.ds(2 * own + i, 1), :].astype(f32)
            out[to, pl.ds(3 * slot + 2, 1), :RK] = hour_rows[pl.ds(hours[t] - first_hour, 1), :]
            row = out[to, ROWS - 1 : ROWS, :]
            row = jnp.where(lane == slot, src_at.astype(f32), row)
            row = jnp.where(lane == 8 + slot, dst_at.astype(f32), row)
            out[to, ROWS - 1 : ROWS, :] = jnp.where(lane == 16, (slot + 1).astype(f32), row)

        alive = t < live
        told = jnp.where(lane == t + 32, jnp.where(alive, src_at, -1).astype(f32), told)
        told = jnp.where(lane == t + 64, dst_at.astype(f32), told)
        return jnp.where(lane == t + 96, rank.astype(f32), told)

    told = lax.fori_loop(0, TILE_CAP, step, jnp.zeros((1, SIDE), f32))
    out[:, ROWS - 1 : ROWS, :] += jnp.broadcast_to(told[None], (GROUPS, 1, SIDE))


def list_kernel(scal, got, lst, seen, staged, meta, sem):
    base = scal[3]
    for o in range(NO):
        seen[o] = 0
    staged[...] = got[:, ROWS - 1, :].astype(i32)
    copy = pltpu.make_async_copy(staged, meta, sem)
    copy.start()
    copy.wait()

    @pl.loop(0, GROUPS)
    def _(g):
        @pl.loop(0, meta[g, 16])
        def _(i):
            dst_at = meta[g, 8 + i]
            to = jnp.bitwise_and(jnp.right_shift(dst_at, 2), NO - 1)
            pos = seen[to] - base
            seen[to] += 1

            @pl.when((pos >= 0) & (pos < PER))
            def _():
                at = to * PER + pos
                lst[at] = meta[g, i]
                lst[LIST + at] = dst_at
                lst[2 * LIST + at] = g * 8 + i

    for o in range(NO):
        lst[3 * LIST + o] = jnp.clip(seen[o] - base, 0, PER)


def each_tile(own, lst, d, work):
    to = jnp.bitwise_and(own + d, NO - 1)

    @pl.loop(0, lst[3 * LIST + to])
    def _(j):
        work(j, PER * to + j)


def slot_row(slot):
    return jnp.right_shift(slot, 3) * ROWS + 3 * jnp.bitwise_and(slot, 7)


def src_pack_kernel(scal, lst, recv, a00, a10, a30, a2t0, a2b0, a01, a11, a31, a2t1, a2b1, *outs):
    own, x_at, c_at = scal[0], scal[1], scal[2]
    sources = (
        ((a00,), (a01,)), ((a10,), (a11,)), ((a2t0, a2b0), (a2t1, a2b1)), ((a30,), (a31,)),
    )
    for d in range(NO):

        def work(j, k):
            src_at = lst[k]
            row = slot_row(lst[2 * LIST + k])
            cols = lane_block(jnp.bitwise_and(src_at, STORED - 1))
            dx = jnp.bitwise_and(jnp.right_shift(src_at, 5) - x_at, NX - 1)
            dc = jnp.bitwise_and(jnp.right_shift(src_at, 4) + c_at, NC - 1)
            for sx in range(NX):
                for sc in range(NC):

                    @pl.when((dx == sx) & (dc == sc))
                    def _():
                        refs = sources[sx][sc]
                        step = RK // len(refs)
                        for h, ref in enumerate(refs):
                            outs[d][j, h * step : (h + 1) * step, :] = ref[:, cols]

            for i in range(3):
                outs[d][j, RK + i : RK + i + 1, :] = recv[pl.ds(row + i, 1), :]

        each_tile(own, lst, d, work)


def tile_kernel(
    scal, lst, a0, a1, a2, a3, b_all, g_out, u0, u1, u2, u3, h0, h1, h2, h3,
    a_in, blocks, g_sum, u_sum, entries, a_sems, in_sems, out_sems,
):
    own = scal[0]
    u_out, h_out = (u0, u1, u2, u3), (h0, h1, h2, h3)
    n = lst[3 * LIST + own]
    shift = jnp.bitwise_and(lax.broadcasted_iota(i32, (32, SIDE), 0), 15)
    left = lax.broadcasted_iota(i32, (1, SIDE), 1) < RK
    ones = jnp.ones((8, SIDE), bf16)
    dg = lambda p, q, dims: lax.dot_general(p, q, (dims, ((), ())), preferred_element_type=f32)

    def place(j):
        dst_at = lst[LIST + PER * own + j]
        return jnp.right_shift(dst_at, 7), lane_block(jnp.bitwise_and(dst_at, STORED // NO - 1))

    def fetch(j):
        z, cols = place(j)
        return pltpu.make_async_copy(b_all.at[z, :, cols], blocks.at[j], in_sems.at[j])

    a_copies = [pltpu.make_async_copy(a, a_in.at[d], a_sems.at[d]) for d, a in enumerate((a0, a1, a2, a3))]
    for copy in a_copies:
        copy.start()

    @pl.loop(0, n)
    def _(j):
        fetch(j).start()

    g_sum[...] = jnp.zeros_like(g_sum)
    for copy in a_copies:
        copy.wait()

    @pl.loop(0, jnp.right_shift(n + 1, 1))
    def _(pair):
        js = 2 * pair, 2 * pair + 1
        fetch(js[0]).wait()

        @pl.when(js[1] < n)
        def _():
            fetch(js[1]).wait()

        terms = []
        for half, j in enumerate(js):
            a_high, a_low = split(jnp.concatenate([a_in[d, j, :RK] for d in range(NO)], axis=0))
            c = jnp.concatenate([as_column(a_in[d, j, RK + 2 : RK + 3, :RK]) for d in range(NO)], axis=0)
            for d in range(NO):
                rows = pl.ds(pl.multiple_of(jnp.bitwise_and(own - d, NO - 1) * 32, 32), 32)
                words = jnp.concatenate(
                    [jnp.broadcast_to(a_in[d, j, RK + i : RK + i + 1, :], (16, SIDE)) for i in range(2)], axis=0
                ).astype(i32)
                entries[half, rows, :] = jnp.bitwise_and(jnp.right_shift(words, shift), 1).astype(f32)
            b_raw = blocks[j]
            b_high, b_low = split(b_raw * c)
            logits = dot3((a_high, a_low), (b_high, b_low), ((0,), (0,)))
            r_high, r_low = split(jax.nn.sigmoid(logits) - entries[half])
            u = dg(
                jnp.concatenate([b_high, b_low], axis=1), jnp.concatenate([r_high, r_high], axis=1), ((1,), (1,))
            ) + dg(b_high, r_low, ((1,), (1,)))
            g = dg(
                jnp.concatenate([a_high, a_low], axis=1), jnp.concatenate([r_high, r_high], axis=0), ((1,), (0,))
            ) + dg(a_high, r_low, ((1,), (0,)))
            h_high, h_low = split(b_raw * g)
            h = (dg(ones, h_high, ((1,), (1,))) + dg(ones, h_low, ((1,), (1,))))[:1]
            for d in range(NO):
                u_sum[d, j] = u[RK * d : RK * (d + 1)]
            for v in range(NO // 2):
                x = h[:, SIDE * v : SIDE * (v + 1)]
                y = jnp.concatenate([x[:, RK:], x[:, :RK]], axis=1)
                h_out[2 * v][pl.ds(j, 1), :] = jnp.where(left, x, y)
                h_out[2 * v + 1][pl.ds(j, 1), :] = jnp.where(left, y, x)
            terms.append(g * c)

        z, cols = place(js[0])
        g_sum[z, :, cols] += terms[0]

        @pl.when(js[1] < n)
        def _():
            z, cols = place(js[1])
            g_sum[z, :, cols] += terms[1]

    copies = [pltpu.make_async_copy(g_sum.at[z], g_out.at[z], out_sems.at[z]) for z in range(NZ)]
    copies += [pltpu.make_async_copy(u_sum.at[d], u_out[d], out_sems.at[NZ + d]) for d in range(NO)]
    for copy in copies:
        copy.start()
    for copy in copies:
        copy.wait()


def hour_pack_kernel(scal, lst, h0, h1, h2, h3, hour):
    hour[...] = jnp.zeros_like(hour)
    upper = jnp.right_shift(lax.broadcasted_iota(i32, (1, SIDE), 1), 6)
    for d, h in enumerate((h0, h1, h2, h3)):

        def work(j, k):
            slot = lst[2 * LIST + k]
            g, i = jnp.right_shift(slot, 3), jnp.bitwise_and(slot, 7)
            cols = lane_block(jnp.right_shift(i, 1))
            hour[g, :, cols] += jnp.where(upper == jnp.bitwise_and(i, 1), h[pl.ds(j, 1), :], 0.0)

        each_tile(scal[0], lst, d, work)


def src_sum_kernel(scal, lst, u0, u1, u2, u3, back, keep, give):
    own, x_at, c_at = scal[0], scal[1], scal[2]
    keep[...] = jnp.zeros_like(keep)
    give[...] = jnp.zeros_like(give)
    for d, u in enumerate((u0, u1, u2, u3)):

        def work(j, k):
            src_at = lst[k]
            cols = lane_block(jnp.bitwise_and(src_at, STORED - 1))
            dx = jnp.bitwise_and(jnp.right_shift(src_at, 5) - x_at, NX - 1)
            dc = jnp.bitwise_and(jnp.right_shift(src_at, 4) + c_at, NC - 1)
            for sc, total in enumerate((keep, give)):

                @pl.when(dc == sc)
                def _():
                    total[dx, :, cols] += u[j]

        each_tile(own, lst, d, work)


def stack_kernel(p0, p1, p2, p3, out):
    for d, p in enumerate((p0, p1, p2, p3)):
        out[RK * d : RK * (d + 1), :] = p[...]


def join_kernel(scal, p0, p1, p2, p3, out):
    for d, p in enumerate((p0, p1, p2, p3)):
        to = jnp.bitwise_and(scal[0] + d, NO - 1)
        out[:, pl.ds(pl.multiple_of(to * PART, PART), PART)] = p[...]


def hour_kernel(scal, hours, where, back, out, both):
    first_hour = scal[1]
    both[...] = jnp.zeros_like(both)
    upper = jnp.right_shift(lax.broadcasted_iota(i32, (1, SIDE), 1), 6)

    @pl.loop(0, TILE_CAP)
    def _(t):
        at = where[t]

        @pl.when(at >= 0)
        def _():
            slot = jnp.bitwise_and(at, 7)
            row = back[jnp.right_shift(at, 3), :, lane_block(jnp.right_shift(slot, 1))]
            both[pl.ds(hours[t] - first_hour, 1), :] += jnp.where(upper == jnp.bitwise_and(slot, 1), row, 0.0)

    out[...] = both[:, :RK] + both[:, RK:]


def shape(*dims, dtype=f32):
    return jax.ShapeDtypeStruct(dims, dtype)


def call(kernel, out_shape, in_specs, args, out_specs=None, scratch=(), vmem=24):
    if out_specs is None:
        out_specs = jax.tree.map(lambda _: VMEM, out_shape)
    return pl.pallas_call(
        kernel, out_shape=out_shape, in_specs=in_specs, out_specs=out_specs,
        scratch_shapes=scratch, compiler_params=pltpu.CompilerParams(vmem_limit_bytes=vmem * MIB),
    )(*args)


def hop(value, axis, size, by):
    if by == 0:
        return value
    return lax.ppermute(value, axis, [(i, (i + by) % size) for i in range(size)])


def per_device(
    src_factor, dst_factor, hour_factor, tile_src, tile_dst, tile_hour, tile_count, src_place, dst_place, tile_bits
):
    z_at, x_at, c_at, own = (lax.axis_index(n).astype(i32) for n in ("z", "x", "c", "own"))
    first_hour = ((z_at * NX + x_at) * NC + c_at) * hour_factor.shape[0]
    live = tile_count[0]
    half = RK // 2

    def part_of(d):
        return jnp.bitwise_and(own + d, NO - 1) * PART

    def one_round(pair_round, base, src_factor, dst_factor):
        src_factor, dst_factor, pair_round = lax.optimization_barrier((src_factor, dst_factor, pair_round))
        with jax.named_scope("slots"):
            scal = jnp.stack([own, first_hour, live, pair_round])
            sent, where = call(
                send_kernel, (shape(GROUPS, ROWS, SIDE), shape(TILE_CAP, dtype=i32)),
                [SMEM] * 6 + [VMEM] * 2,
                (scal, tile_src, tile_dst, tile_hour, src_place, dst_place, tile_bits, hour_factor),
                out_specs=(VMEM, SMEM), scratch=[pltpu.SMEM((GROUPS,), i32)],
            )
        with jax.named_scope("gather_dst"):
            parts = [
                hop(lax.dynamic_slice(dst_factor, (0, part_of(d)), (RK, PART)), "own", NO, d) for d in range(NO)
            ]
            parts, sent = lax.optimization_barrier((parts, sent))
            b_mine = call(stack_kernel, shape(RANK, PART), [VMEM] * NO, parts)
            b_all = lax.all_gather(b_mine, "z", axis=0)
        with jax.named_scope("slots"):
            got = lax.all_to_all(sent, SLAB, 0, 0)
            rows = got.reshape(GROUPS * ROWS, SIDE)
            told = got[:, ROWS - 1].astype(i32)
        with jax.named_scope("gather_src"):
            stored, _ = lax.optimization_barrier((src_factor, b_mine))
            up = hop(stored, "x", NX, 1)
            down = hop(stored, "x", NX, -1)
            far_top = hop(up[:half], "x", NX, 1)
            far_bottom = hop(down[half:], "x", NX, -1)
            mine = (stored, down, up, far_top, far_bottom)
            a_all = mine + tuple(hop(v, "c", NC, 1) for v in mine)
        at = jnp.stack([own, x_at, c_at, base])
        with jax.named_scope("list"):
            lst = call(
                list_kernel, shape(3 * LIST + 8, dtype=i32), [SMEM, VMEM], (at, got), out_specs=SMEM,
                scratch=[
                    pltpu.SMEM((NO,), i32), pltpu.VMEM((GROUPS, SIDE), i32), pltpu.SMEM((GROUPS, SIDE), i32),
                    pltpu.SemaphoreType.DMA,
                ],
            )
        with jax.named_scope("src_exchange"):
            a_out = call(
                src_pack_kernel, (shape(PER, XROWS, SIDE),) * NO, [SMEM] * 2 + [VMEM] * 11, (at, lst, rows) + a_all
            )
            a_in = [hop(v, "own", NO, d) for d, v in enumerate(a_out)]
        with jax.named_scope("tiles"):
            g_sum, *out = call(
                tile_kernel,
                (shape(NZ, RANK, PART),) + (shape(PER, RK, SIDE),) * NO + (shape(PER, SIDE),) * NO,
                [SMEM] * 2 + [HBM] * (NO + 1), (at, lst, *a_in, b_all), out_specs=(HBM,) * (1 + NO) + (VMEM,) * NO,
                scratch=[
                    pltpu.VMEM((NO, PER, XROWS, SIDE), f32), pltpu.VMEM((PER, RANK, SIDE), f32),
                    pltpu.VMEM((NZ, RANK, PART), f32), pltpu.VMEM((NO, PER, RK, SIDE), f32),
                    pltpu.VMEM((2, SIDE, SIDE), f32), pltpu.SemaphoreType.DMA((NO,)), pltpu.SemaphoreType.DMA((PER,)),
                    pltpu.SemaphoreType.DMA((NZ + NO,)),
                ],
                vmem=60,
            )
        with jax.named_scope("hours"):
            h = [hop(v, "own", NO, -d) for d, v in enumerate(out[NO:])]
            hour_terms = call(hour_pack_kernel, shape(GROUPS, 1, 3 * SIDE), [SMEM] * 2 + [VMEM] * NO, (at, lst, *h))
            back = lax.all_to_all(hour_terms, SLAB, 0, 0)
            grad_hour = call(
                hour_kernel, shape(*hour_factor.shape), [SMEM] * 3 + [VMEM], (scal, tile_hour, where, back),
                scratch=[pltpu.VMEM((hour_factor.shape[0], SIDE), f32)],
            )
        with jax.named_scope("src_back"):
            u_out, _ = lax.optimization_barrier((out[:NO], h))
            u = [hop(v, "own", NO, -d) for d, v in enumerate(u_out)]
            keep, give = call(
                src_sum_kernel, (shape(NX, RK, STORED * SIDE),) * 2, [SMEM] * 2 + [VMEM] * NO + [ANY],
                (at, lst, *u, back),
            )
            s = keep + hop(give, "c", NC, 1)
            top = hop(s[2, :half], "x", NX, 1)
            bottom = hop(s[2, half:], "x", NX, -1)
            one = hop(jnp.concatenate([s[1, :half] + top, s[1, half:]]), "x", NX, 1)
            three = hop(jnp.concatenate([s[3, :half], s[3, half:] + bottom]), "x", NX, -1)
            grad_src = s[0] + one + three
        with jax.named_scope("dst_back"):
            g_part = lax.psum_scatter(g_sum, "z", scatter_dimension=0)
            pieces = [hop(g_part[RK * d : RK * (d + 1)], "own", NO, -d) for d in range(NO)]
            grad_dst = call(join_kernel, shape(*dst_factor.shape), [SMEM] + [VMEM] * NO, (at, *pieces))
        return (grad_src, grad_dst, grad_hour), told

    zero = jnp.zeros((), i32)
    grads, told = one_round(zero, zero, src_factor, dst_factor)

    src_at, dst_at, rank = (told[:, 32 * i : 32 * i + TILE_CAP].reshape(-1) for i in range(1, 4))
    worker = (src_at // 128) * 32 + (dst_at // STORED) % 8 * NO + dst_at % STORED // NO
    alive = src_at >= 0

    def busiest(pair_round):
        here = alive & (rank // SLOTS == pair_round)
        counts = jnp.sum((worker[None, :] == jnp.arange(GROUPS * NO, dtype=i32)[:, None]) & here[None, :], axis=1)
        return jnp.max(counts.astype(i32))

    def following(pair_round, base):
        more = base + PER < busiest(pair_round)
        return jnp.where(more, pair_round, pair_round + 1), jnp.where(more, base + PER, 0)

    def body(state):
        pair_round, base, sums = state
        terms, _ = one_round(pair_round, base, src_factor, dst_factor)
        return following(pair_round, base) + (jax.tree.map(jnp.add, sums, terms),)

    top_rank = jnp.max(jnp.where(alive, rank, -1))
    last = lax.while_loop(lambda state: top_rank >= state[0] * SLOTS, body, following(zero, zero) + (grads,))
    return last[2]


def solution(mesh):
    fine = Mesh(mesh.devices.reshape(NZ, NX, NC, NO), SLAB + ("own",))
    return jax.shard_map(
        per_device,
        mesh=fine,
        in_specs=(
            P("own", SLAB), P("own", SLAB), P(SLAB, "own"), P(SLAB), P(SLAB), P(SLAB), P(SLAB), P(), P(),
            P(SLAB, None, None),
        ),
        out_specs=(P("own", SLAB), P("own", SLAB), P(SLAB, "own")),
        check_vma=False,
    )
```

```python
import jax
import jax.numpy as jnp
from jax import lax
from jax.experimental import pallas as pl
from jax.experimental.pallas import tpu as pltpu
from jax.sharding import Mesh, PartitionSpec as P

NZ, NX, NC, NO = 8, 4, 2, 4
SLAB = ("z", "x", "c")
GROUPS = 64
TILE_CAP = 30
SIDE = 128
RK = 64
RANK = RK * NO
STORED = 16
PART = STORED // NO * SIDE
SLOTS = 5
ROWS = 3 * SLOTS + 1
PER = 15
LIST = NO * PER
XROWS = RK + 8
VMEM = pl.BlockSpec(memory_space=pltpu.VMEM)
SMEM = pl.BlockSpec(memory_space=pltpu.SMEM)
ANY = pl.BlockSpec(memory_space=pl.ANY)
HBM = pl.BlockSpec(memory_space=pltpu.HBM)
f32, bf16, i32 = jnp.float32, jnp.bfloat16, jnp.int32
MIB = 1024 * 1024


def lane_block(within):
    return pl.ds(pl.multiple_of(within * SIDE, SIDE), SIDE)


def split(x):
    hi = x.astype(bf16)
    return hi, (x - hi.astype(f32)).astype(bf16)


def dot3(a, b, dims):
    dg = lambda p, q: lax.dot_general(p, q, (dims, ((), ())), preferred_element_type=f32)
    return dg(a[0], b[0]) + (dg(a[0], b[1]) + dg(a[1], b[0]))


def as_column(row):
    return jnp.broadcast_to(row, (SIDE, RK)).T


def send_kernel(scal, src_ids, dst_ids, hours, src_place, dst_place, bits, hour_rows, out, where, count):
    own, first_hour, live, pair_round = scal[0], scal[1], scal[2], scal[3]

    @pl.loop(0, GROUPS)
    def _(g):
        count[g] = 0

    out[...] = jnp.zeros_like(out)
    lane = lax.broadcasted_iota(i32, (1, SIDE), 1)

    def step(t, told):
        src_at = src_place[src_ids[t]]
        dst_at = dst_place[dst_ids[t]]
        to = jnp.right_shift(src_at, 7) * 8 + jnp.bitwise_and(jnp.right_shift(dst_at, 4), 7)
        rank = count[to]
        slot = rank - pair_round * SLOTS
        here = (t < live) & (slot >= 0) & (slot < SLOTS)
        where[t] = jnp.where(here, to * 8 + slot, -1)

        @pl.when(t < live)
        def _():
            count[to] = rank + 1

        @pl.when(here)
        def _():
            for i in range(2):
                out[to, pl.ds(3 * slot + i, 1), :] = bits[t, pl.ds(2 * own + i, 1), :].astype(f32)
            out[to, pl.ds(3 * slot + 2, 1), :RK] = hour_rows[pl.ds(hours[t] - first_hour, 1), :]
            row = out[to, ROWS - 1 : ROWS, :]
            row = jnp.where(lane == slot, src_at.astype(f32), row)
            row = jnp.where(lane == 8 + slot, dst_at.astype(f32), row)
            out[to, ROWS - 1 : ROWS, :] = jnp.where(lane == 16, (slot + 1).astype(f32), row)

        alive = t < live
        told = jnp.where(lane == t + 32, jnp.where(alive, src_at, -1).astype(f32), told)
        told = jnp.where(lane == t + 64, dst_at.astype(f32), told)
        return jnp.where(lane == t + 96, rank.astype(f32), told)

    told = lax.fori_loop(0, TILE_CAP, step, jnp.zeros((1, SIDE), f32))
    out[:, ROWS - 1 : ROWS, :] += jnp.broadcast_to(told[None], (GROUPS, 1, SIDE))


def list_kernel(scal, got, lst, seen, staged, meta, sem):
    base = scal[3]
    for o in range(NO):
        seen[o] = 0
    staged[...] = got[:, ROWS - 1, :].astype(i32)
    copy = pltpu.make_async_copy(staged, meta, sem)
    copy.start()
    copy.wait()

    @pl.loop(0, GROUPS)
    def _(g):
        @pl.loop(0, meta[g, 16])
        def _(i):
            dst_at = meta[g, 8 + i]
            to = jnp.bitwise_and(jnp.right_shift(dst_at, 2), NO - 1)
            pos = seen[to] - base
            seen[to] += 1

            @pl.when((pos >= 0) & (pos < PER))
            def _():
                at = to * PER + pos
                lst[at] = meta[g, i]
                lst[LIST + at] = dst_at
                lst[2 * LIST + at] = g * 8 + i

    for o in range(NO):
        lst[3 * LIST + o] = jnp.clip(seen[o] - base, 0, PER)


def each_tile(own, lst, d, work):
    to = jnp.bitwise_and(own + d, NO - 1)

    @pl.loop(0, lst[3 * LIST + to])
    def _(j):
        work(j, PER * to + j)


def slot_row(slot):
    return jnp.right_shift(slot, 3) * ROWS + 3 * jnp.bitwise_and(slot, 7)


def src_pack_kernel(scal, lst, recv, a00, a10, a30, a2t0, a2b0, a01, a11, a31, a2t1, a2b1, *outs):
    own, x_at, c_at = scal[0], scal[1], scal[2]
    sources = (
        ((a00,), (a01,)), ((a10,), (a11,)), ((a2t0, a2b0), (a2t1, a2b1)), ((a30,), (a31,)),
    )
    for d in range(NO):

        def work(j, k):
            src_at = lst[k]
            row = slot_row(lst[2 * LIST + k])
            cols = lane_block(jnp.bitwise_and(src_at, STORED - 1))
            dx = jnp.bitwise_and(jnp.right_shift(src_at, 5) - x_at, NX - 1)
            dc = jnp.bitwise_and(jnp.right_shift(src_at, 4) + c_at, NC - 1)
            for sx in range(NX):
                for sc in range(NC):

                    @pl.when((dx == sx) & (dc == sc))
                    def _():
                        refs = sources[sx][sc]
                        step = RK // len(refs)
                        for h, ref in enumerate(refs):
                            outs[d][j, h * step : (h + 1) * step, :] = ref[:, cols]

            for i in range(3):
                outs[d][j, RK + i : RK + i + 1, :] = recv[pl.ds(row + i, 1), :]

        each_tile(own, lst, d, work)


def tile_kernel(
    scal, lst, a0, a1, a2, a3, b_all, g_out, u0, u1, u2, u3, h0, h1, h2, h3,
    blocks, g_sum, u_sum, entries, in_sems, g_sems, u_sems,
):
    own = scal[0]
    a_in, u_out, h_out = (a0, a1, a2, a3), (u0, u1, u2, u3), (h0, h1, h2, h3)
    n = lst[3 * LIST + own]
    shift = jnp.bitwise_and(lax.broadcasted_iota(i32, (32, SIDE), 0), 15)
    left = lax.broadcasted_iota(i32, (1, SIDE), 1) < RK
    ones = jnp.ones((8, SIDE), bf16)
    dg = lambda p, q, dims: lax.dot_general(p, q, (dims, ((), ())), preferred_element_type=f32)

    def place(j):
        dst_at = lst[LIST + PER * own + j]
        return jnp.right_shift(dst_at, 7), lane_block(jnp.bitwise_and(dst_at, STORED // NO - 1))

    def fetch(j):
        z, cols = place(j)
        return pltpu.make_async_copy(b_all.at[z, :, cols], blocks.at[j], in_sems.at[j])

    def leave(j):
        return [pltpu.make_async_copy(u_sum.at[d, j], u_out[d].at[j], u_sems.at[d, j]) for d in range(NO)]

    @pl.loop(0, n)
    def _(j):
        fetch(j).start()

    g_sum[...] = jnp.zeros_like(g_sum)
    @pl.loop(0, jnp.right_shift(n + 1, 1))
    def _(pair):
        js = 2 * pair, jnp.minimum(2 * pair + 1, PER - 1)
        both = 2 * pair + 1 < n
        fetch(js[0]).wait()

        @pl.when(both)
        def _():
            fetch(js[1]).wait()

        terms = []
        for half, j in enumerate(js):
            a_high, a_low = split(jnp.concatenate([a_in[d][j, :RK] for d in range(NO)], axis=0))
            c = jnp.concatenate([as_column(a_in[d][j, RK + 2 : RK + 3, :RK]) for d in range(NO)], axis=0)
            for d in range(NO):
                rows = pl.ds(pl.multiple_of(jnp.bitwise_and(own - d, NO - 1) * 32, 32), 32)
                words = jnp.concatenate(
                    [jnp.broadcast_to(a_in[d][j, RK + i : RK + i + 1, :], (16, SIDE)) for i in range(2)], axis=0
                ).astype(i32)
                entries[half, rows, :] = jnp.bitwise_and(jnp.right_shift(words, shift), 1).astype(f32)
            b_raw = blocks[j]
            b_high, b_low = split(b_raw * c)
            logits = dot3((a_high, a_low), (b_high, b_low), ((0,), (0,)))
            r_high, r_low = split(jax.nn.sigmoid(logits) - entries[half])
            u = dg(
                jnp.concatenate([b_high, b_low], axis=1), jnp.concatenate([r_high, r_high], axis=1), ((1,), (1,))
            ) + dg(b_high, r_low, ((1,), (1,)))
            g = dg(
                jnp.concatenate([a_high, a_low], axis=1), jnp.concatenate([r_high, r_high], axis=0), ((1,), (0,))
            ) + dg(a_high, r_low, ((1,), (0,)))
            h_high, h_low = split(b_raw * g)
            h = (dg(ones, h_high, ((1,), (1,))) + dg(ones, h_low, ((1,), (1,))))[:1]
            for d in range(NO):
                u_sum[d, j] = u[RK * d : RK * (d + 1)]
            for v in range(NO // 2):
                x = h[:, SIDE * v : SIDE * (v + 1)]
                y = jnp.concatenate([x[:, RK:], x[:, :RK]], axis=1)
                h_out[2 * v][pl.ds(j, 1), :] = jnp.where(left, x, y)
                h_out[2 * v + 1][pl.ds(j, 1), :] = jnp.where(left, y, x)
            terms.append(g * c)

        def finish(half):
            z, cols = place(js[half])
            g_sum[z, :, cols] += terms[half]
            for copy in leave(js[half]):
                copy.start()

        finish(0)
        pl.when(both)(lambda: finish(1))

    copies = [pltpu.make_async_copy(g_sum.at[z], g_out.at[z], g_sems.at[z]) for z in range(NZ)]
    for copy in copies:
        copy.start()

    @pl.loop(0, n)
    def _(j):
        for copy in leave(j):
            copy.wait()

    for copy in copies:
        copy.wait()


def hour_pack_kernel(scal, lst, h0, h1, h2, h3, hour):
    hour[...] = jnp.zeros_like(hour)
    upper = jnp.right_shift(lax.broadcasted_iota(i32, (1, SIDE), 1), 6)
    for d, h in enumerate((h0, h1, h2, h3)):

        def work(j, k):
            slot = lst[2 * LIST + k]
            g, i = jnp.right_shift(slot, 3), jnp.bitwise_and(slot, 7)
            cols = lane_block(jnp.right_shift(i, 1))
            hour[g, :, cols] += jnp.where(upper == jnp.bitwise_and(i, 1), h[pl.ds(j, 1), :], 0.0)

        each_tile(scal[0], lst, d, work)


def src_sum_kernel(scal, lst, u0, u1, u2, u3, back, keep, give):
    own, x_at, c_at = scal[0], scal[1], scal[2]
    keep[...] = jnp.zeros_like(keep)
    give[...] = jnp.zeros_like(give)
    for d, u in enumerate((u0, u1, u2, u3)):

        def work(j, k):
            src_at = lst[k]
            cols = lane_block(jnp.bitwise_and(src_at, STORED - 1))
            dx = jnp.bitwise_and(jnp.right_shift(src_at, 5) - x_at, NX - 1)
            dc = jnp.bitwise_and(jnp.right_shift(src_at, 4) + c_at, NC - 1)
            for sc, total in enumerate((keep, give)):

                @pl.when(dc == sc)
                def _():
                    total[dx, :, cols] += u[j]

        each_tile(own, lst, d, work)


def stack_kernel(p0, p1, p2, p3, out):
    for d, p in enumerate((p0, p1, p2, p3)):
        out[RK * d : RK * (d + 1), :] = p[...]


def join_kernel(scal, p0, p1, p2, p3, out):
    for d, p in enumerate((p0, p1, p2, p3)):
        to = jnp.bitwise_and(scal[0] + d, NO - 1)
        out[:, pl.ds(pl.multiple_of(to * PART, PART), PART)] = p[...]


def hour_kernel(scal, hours, where, back, out, both):
    first_hour = scal[1]
    both[...] = jnp.zeros_like(both)
    upper = jnp.right_shift(lax.broadcasted_iota(i32, (1, SIDE), 1), 6)

    @pl.loop(0, TILE_CAP)
    def _(t):
        at = where[t]

        @pl.when(at >= 0)
        def _():
            slot = jnp.bitwise_and(at, 7)
            row = back[jnp.right_shift(at, 3), :, lane_block(jnp.right_shift(slot, 1))]
            both[pl.ds(hours[t] - first_hour, 1), :] += jnp.where(upper == jnp.bitwise_and(slot, 1), row, 0.0)

    out[...] = both[:, :RK] + both[:, RK:]


def shape(*dims, dtype=f32):
    return jax.ShapeDtypeStruct(dims, dtype)


def call(kernel, out_shape, in_specs, args, out_specs=None, scratch=(), vmem=24):
    if out_specs is None:
        out_specs = jax.tree.map(lambda _: VMEM, out_shape)
    return pl.pallas_call(
        kernel, out_shape=out_shape, in_specs=in_specs, out_specs=out_specs,
        scratch_shapes=scratch, compiler_params=pltpu.CompilerParams(vmem_limit_bytes=vmem * MIB),
    )(*args)


def hop(value, axis, size, by):
    if by == 0:
        return value
    return lax.ppermute(value, axis, [(i, (i + by) % size) for i in range(size)])


def per_device(
    src_factor, dst_factor, hour_factor, tile_src, tile_dst, tile_hour, tile_count, src_place, dst_place, tile_bits
):
    z_at, x_at, c_at, own = (lax.axis_index(n).astype(i32) for n in ("z", "x", "c", "own"))
    first_hour = ((z_at * NX + x_at) * NC + c_at) * hour_factor.shape[0]
    live = tile_count[0]
    half = RK // 2

    def part_of(d):
        return jnp.bitwise_and(own + d, NO - 1) * PART

    def one_round(pair_round, base, src_factor, dst_factor):
        src_factor, dst_factor, pair_round = lax.optimization_barrier((src_factor, dst_factor, pair_round))
        with jax.named_scope("slots"):
            scal = jnp.stack([own, first_hour, live, pair_round])
            sent, where = call(
                send_kernel, (shape(GROUPS, ROWS, SIDE), shape(TILE_CAP, dtype=i32)),
                [SMEM] * 6 + [VMEM] * 2,
                (scal, tile_src, tile_dst, tile_hour, src_place, dst_place, tile_bits, hour_factor),
                out_specs=(VMEM, SMEM), scratch=[pltpu.SMEM((GROUPS,), i32)],
            )
        with jax.named_scope("gather_dst"):
            parts = [
                hop(lax.dynamic_slice(dst_factor, (0, part_of(d)), (RK, PART)), "own", NO, d) for d in range(NO)
            ]
            parts, sent = lax.optimization_barrier((parts, sent))
            b_mine = call(stack_kernel, shape(RANK, PART), [VMEM] * NO, parts)
            b_all = lax.all_gather(b_mine, "z", axis=0)
        with jax.named_scope("slots"):
            got = lax.all_to_all(sent, SLAB, 0, 0)
            rows = got.reshape(GROUPS * ROWS, SIDE)
            told = got[:, ROWS - 1].astype(i32)
        with jax.named_scope("gather_src"):
            stored, _ = lax.optimization_barrier((src_factor, b_mine))
            up = hop(stored, "x", NX, 1)
            down = hop(stored, "x", NX, -1)
            far_top = hop(up[:half], "x", NX, 1)
            far_bottom = hop(down[half:], "x", NX, -1)
            mine = (stored, down, up, far_top, far_bottom)
            a_all = mine + tuple(hop(v, "c", NC, 1) for v in mine)
        at = jnp.stack([own, x_at, c_at, base])
        with jax.named_scope("list"):
            lst = call(
                list_kernel, shape(3 * LIST + 8, dtype=i32), [SMEM, VMEM], (at, got), out_specs=SMEM,
                scratch=[
                    pltpu.SMEM((NO,), i32), pltpu.VMEM((GROUPS, SIDE), i32), pltpu.SMEM((GROUPS, SIDE), i32),
                    pltpu.SemaphoreType.DMA,
                ],
            )
        with jax.named_scope("src_exchange"):
            a_out = call(
                src_pack_kernel, (shape(PER, XROWS, SIDE),) * NO, [SMEM] * 2 + [VMEM] * 11, (at, lst, rows) + a_all
            )
            a_in = [hop(v, "own", NO, d) for d, v in enumerate(a_out)]
        with jax.named_scope("tiles"):
            g_sum, *out = call(
                tile_kernel,
                (shape(NZ, RANK, PART),) + (shape(PER, RK, SIDE),) * NO + (shape(PER, SIDE),) * NO,
                [SMEM] * 2 + [VMEM] * NO + [HBM], (at, lst, *a_in, b_all), out_specs=(HBM,) * (1 + NO) + (VMEM,) * NO,
                scratch=[
                    pltpu.VMEM((PER, RANK, SIDE), f32), pltpu.VMEM((NZ, RANK, PART), f32),
                    pltpu.VMEM((NO, PER, RK, SIDE), f32), pltpu.VMEM((2, SIDE, SIDE), f32),
                    pltpu.SemaphoreType.DMA((PER,)), pltpu.SemaphoreType.DMA((NZ,)),
                    pltpu.SemaphoreType.DMA((NO, PER)),
                ],
                vmem=52,
            )
        with jax.named_scope("hours"):
            h = [hop(v, "own", NO, -d) for d, v in enumerate(out[NO:])]
            hour_terms = call(hour_pack_kernel, shape(GROUPS, 1, 3 * SIDE), [SMEM] * 2 + [VMEM] * NO, (at, lst, *h))
            back = lax.all_to_all(hour_terms, SLAB, 0, 0)
            grad_hour = call(
                hour_kernel, shape(*hour_factor.shape), [SMEM] * 3 + [VMEM], (scal, tile_hour, where, back),
                scratch=[pltpu.VMEM((hour_factor.shape[0], SIDE), f32)],
            )
        with jax.named_scope("src_back"):
            u_out, _ = lax.optimization_barrier((out[:NO], h))
            u = [hop(v, "own", NO, -d) for d, v in enumerate(u_out)]
            keep, give = call(
                src_sum_kernel, (shape(NX, RK, STORED * SIDE),) * 2, [SMEM] * 2 + [VMEM] * NO + [ANY],
                (at, lst, *u, back),
            )
            s = keep + hop(give, "c", NC, 1)
            far_top = hop(hop(s[2, :half], "x", NX, 1), "x", NX, 1)
            far_bottom = hop(hop(s[2, half:], "x", NX, -1), "x", NX, -1)
            near = s[0] + hop(s[1], "x", NX, 1) + hop(s[3], "x", NX, -1)
            grad_src = near + jnp.concatenate([far_top, far_bottom])
        with jax.named_scope("dst_back"):
            g_part = lax.psum_scatter(g_sum, "z", scatter_dimension=0)
            pieces = [hop(g_part[RK * d : RK * (d + 1)], "own", NO, -d) for d in range(NO)]
            grad_dst = call(join_kernel, shape(*dst_factor.shape), [SMEM] + [VMEM] * NO, (at, *pieces))
        return (grad_src, grad_dst, grad_hour), told

    zero = jnp.zeros((), i32)
    grads, told = one_round(zero, zero, src_factor, dst_factor)

    src_at, dst_at, rank = (told[:, 32 * i : 32 * i + TILE_CAP].reshape(-1) for i in range(1, 4))
    worker = (src_at // 128) * 32 + (dst_at // STORED) % 8 * NO + dst_at % STORED // NO
    alive = src_at >= 0

    def busiest(pair_round):
        here = alive & (rank // SLOTS == pair_round)
        counts = jnp.sum((worker[None, :] == jnp.arange(GROUPS * NO, dtype=i32)[:, None]) & here[None, :], axis=1)
        return jnp.max(counts.astype(i32))

    def following(pair_round, base):
        more = base + PER < busiest(pair_round)
        return jnp.where(more, pair_round, pair_round + 1), jnp.where(more, base + PER, 0)

    def body(state):
        pair_round, base, sums = state
        terms, _ = one_round(pair_round, base, src_factor, dst_factor)
        return following(pair_round, base) + (jax.tree.map(jnp.add, sums, terms),)

    top_rank = jnp.max(jnp.where(alive, rank, -1))
    last = lax.while_loop(lambda state: top_rank >= state[0] * SLOTS, body, following(zero, zero) + (grads,))
    return last[2]


def solution(mesh):
    fine = Mesh(mesh.devices.reshape(NZ, NX, NC, NO), SLAB + ("own",))
    return jax.shard_map(
        per_device,
        mesh=fine,
        in_specs=(
            P("own", SLAB), P("own", SLAB), P(SLAB, "own"), P(SLAB), P(SLAB), P(SLAB), P(SLAB), P(), P(),
            P(SLAB, None, None),
        ),
        out_specs=(P("own", SLAB), P("own", SLAB), P(SLAB, "own")),
        check_vma=False,
    )
```

```python
import jax
import jax.numpy as jnp
from jax import lax
from jax.experimental import pallas as pl
from jax.experimental.pallas import tpu as pltpu
from jax.sharding import Mesh, PartitionSpec as P

NZ, NX, NC, NO = 8, 4, 2, 4
SLAB = ("z", "x", "c")
GROUPS = 64
TILE_CAP = 30
SIDE = 128
RK = 64
RANK = RK * NO
STORED = 16
PART = STORED // NO * SIDE
SLOTS = 5
ROWS = 3 * SLOTS + 1
PER = 15
LIST = NO * PER
XROWS = RK + 8
VMEM = pl.BlockSpec(memory_space=pltpu.VMEM)
SMEM = pl.BlockSpec(memory_space=pltpu.SMEM)
ANY = pl.BlockSpec(memory_space=pl.ANY)
HBM = pl.BlockSpec(memory_space=pltpu.HBM)
f32, bf16, i32 = jnp.float32, jnp.bfloat16, jnp.int32
MIB = 1024 * 1024


def lane_block(within):
    return pl.ds(pl.multiple_of(within * SIDE, SIDE), SIDE)


def split(x):
    hi = x.astype(bf16)
    return hi, (x - hi.astype(f32)).astype(bf16)


def dot3(a, b, dims):
    dg = lambda p, q: lax.dot_general(p, q, (dims, ((), ())), preferred_element_type=f32)
    return dg(a[0], b[0]) + (dg(a[0], b[1]) + dg(a[1], b[0]))


def as_column(row):
    return jnp.broadcast_to(row, (SIDE, RK)).T


def send_kernel(scal, src_ids, dst_ids, hours, src_place, dst_place, bits, hour_rows, out, where, count):
    own, first_hour, live, pair_round = scal[0], scal[1], scal[2], scal[3]

    @pl.loop(0, GROUPS)
    def _(g):
        count[g] = 0

    out[...] = jnp.zeros_like(out)
    lane = lax.broadcasted_iota(i32, (1, SIDE), 1)

    def step(t, told):
        src_at = src_place[src_ids[t]]
        dst_at = dst_place[dst_ids[t]]
        to = jnp.right_shift(src_at, 7) * 8 + jnp.bitwise_and(jnp.right_shift(dst_at, 4), 7)
        rank = count[to]
        slot = rank - pair_round * SLOTS
        here = (t < live) & (slot >= 0) & (slot < SLOTS)
        where[t] = jnp.where(here, to * 8 + slot, -1)

        @pl.when(t < live)
        def _():
            count[to] = rank + 1

        @pl.when(here)
        def _():
            for i in range(2):
                out[to, pl.ds(3 * slot + i, 1), :] = bits[t, pl.ds(2 * own + i, 1), :].astype(f32)
            out[to, pl.ds(3 * slot + 2, 1), :RK] = hour_rows[pl.ds(hours[t] - first_hour, 1), :]
            row = out[to, ROWS - 1 : ROWS, :]
            row = jnp.where(lane == slot, src_at.astype(f32), row)
            row = jnp.where(lane == 8 + slot, dst_at.astype(f32), row)
            out[to, ROWS - 1 : ROWS, :] = jnp.where(lane == 16, (slot + 1).astype(f32), row)

        alive = t < live
        told = jnp.where(lane == t + 32, jnp.where(alive, src_at, -1).astype(f32), told)
        told = jnp.where(lane == t + 64, dst_at.astype(f32), told)
        return jnp.where(lane == t + 96, rank.astype(f32), told)

    told = lax.fori_loop(0, TILE_CAP, step, jnp.zeros((1, SIDE), f32))
    out[:, ROWS - 1 : ROWS, :] += jnp.broadcast_to(told[None], (GROUPS, 1, SIDE))


def list_kernel(scal, got, lst, seen, staged, meta, sem):
    base = scal[3]
    for o in range(NO):
        seen[o] = 0
    staged[...] = got[:, ROWS - 1, :].astype(i32)
    copy = pltpu.make_async_copy(staged, meta, sem)
    copy.start()
    copy.wait()

    @pl.loop(0, GROUPS)
    def _(g):
        @pl.loop(0, meta[g, 16])
        def _(i):
            dst_at = meta[g, 8 + i]
            to = jnp.bitwise_and(jnp.right_shift(dst_at, 2), NO - 1)
            pos = seen[to] - base
            seen[to] += 1

            @pl.when((pos >= 0) & (pos < PER))
            def _():
                at = to * PER + pos
                lst[at] = meta[g, i]
                lst[LIST + at] = dst_at
                lst[2 * LIST + at] = g * 8 + i

    for o in range(NO):
        lst[3 * LIST + o] = jnp.clip(seen[o] - base, 0, PER)


def each_tile(own, lst, d, work):
    to = jnp.bitwise_and(own + d, NO - 1)

    @pl.loop(0, lst[3 * LIST + to])
    def _(j):
        work(j, PER * to + j)


def slot_row(slot):
    return jnp.right_shift(slot, 3) * ROWS + 3 * jnp.bitwise_and(slot, 7)


def src_pack_kernel(scal, lst, recv, a00, a10, a30, a2t0, a2b0, a01, a11, a31, a2t1, a2b1, *outs):
    own, x_at, c_at = scal[0], scal[1], scal[2]
    sources = (
        ((a00,), (a01,)), ((a10,), (a11,)), ((a2t0, a2b0), (a2t1, a2b1)), ((a30,), (a31,)),
    )
    for d in range(NO):

        def work(j, k):
            src_at = lst[k]
            row = slot_row(lst[2 * LIST + k])
            cols = lane_block(jnp.bitwise_and(src_at, STORED - 1))
            dx = jnp.bitwise_and(jnp.right_shift(src_at, 5) - x_at, NX - 1)
            dc = jnp.bitwise_and(jnp.right_shift(src_at, 4) + c_at, NC - 1)
            for sx in range(NX):
                for sc in range(NC):

                    @pl.when((dx == sx) & (dc == sc))
                    def _():
                        refs = sources[sx][sc]
                        step = RK // len(refs)
                        for h, ref in enumerate(refs):
                            outs[d][j, h * step : (h + 1) * step, :] = ref[:, cols]

            for i in range(3):
                outs[d][j, RK + i : RK + i + 1, :] = recv[pl.ds(row + i, 1), :]

        each_tile(own, lst, d, work)


def tile_kernel(
    scal, lst, a0, a1, a2, a3, b_all, g_out, u0, u1, u2, u3, h0, h1, h2, h3,
    blocks, g_sum, u_sum, entries, in_sems, g_sems, u_sems,
):
    own = scal[0]
    a_in, u_out, h_out = (a0, a1, a2, a3), (u0, u1, u2, u3), (h0, h1, h2, h3)
    n = lst[3 * LIST + own]
    shift = jnp.bitwise_and(lax.broadcasted_iota(i32, (32, SIDE), 0), 15)
    left = lax.broadcasted_iota(i32, (1, SIDE), 1) < RK
    ones = jnp.ones((8, SIDE), bf16)
    dg = lambda p, q, dims: lax.dot_general(p, q, (dims, ((), ())), preferred_element_type=f32)

    def place(j):
        dst_at = lst[LIST + PER * own + j]
        return jnp.right_shift(dst_at, 7), lane_block(jnp.bitwise_and(dst_at, STORED // NO - 1))

    def fetch(j):
        z, cols = place(j)
        return pltpu.make_async_copy(b_all.at[z, :, cols], blocks.at[j], in_sems.at[j])

    def leave(j):
        return [pltpu.make_async_copy(u_sum.at[d, j], u_out[d].at[j], u_sems.at[d, j]) for d in range(NO)]

    @pl.loop(0, n)
    def _(j):
        fetch(j).start()

    g_sum[...] = jnp.zeros_like(g_sum)
    @pl.loop(0, jnp.right_shift(n + 1, 1))
    def _(pair):
        js = 2 * pair, jnp.minimum(2 * pair + 1, PER - 1)
        both = 2 * pair + 1 < n
        fetch(js[0]).wait()

        @pl.when(both)
        def _():
            fetch(js[1]).wait()

        terms = []
        for half, j in enumerate(js):
            a_high, a_low = split(jnp.concatenate([a_in[d][j, :RK] for d in range(NO)], axis=0))
            c = jnp.concatenate([as_column(a_in[d][j, RK + 2 : RK + 3, :RK]) for d in range(NO)], axis=0)
            for d in range(NO):
                rows = pl.ds(pl.multiple_of(jnp.bitwise_and(own - d, NO - 1) * 32, 32), 32)
                words = jnp.concatenate(
                    [jnp.broadcast_to(a_in[d][j, RK + i : RK + i + 1, :], (16, SIDE)) for i in range(2)], axis=0
                ).astype(i32)
                entries[half, rows, :] = jnp.bitwise_and(jnp.right_shift(words, shift), 1).astype(f32)
            b_raw = blocks[j]
            b_high, b_low = split(b_raw * c)
            logits = dot3((a_high, a_low), (b_high, b_low), ((0,), (0,)))
            r_high, r_low = split(jax.nn.sigmoid(logits) - entries[half])
            u = dg(
                jnp.concatenate([b_high, b_low], axis=1), jnp.concatenate([r_high, r_high], axis=1), ((1,), (1,))
            ) + dg(b_high, r_low, ((1,), (1,)))
            g = dg(
                jnp.concatenate([a_high, a_low], axis=1), jnp.concatenate([r_high, r_high], axis=0), ((1,), (0,))
            ) + dg(a_high, r_low, ((1,), (0,)))
            h_high, h_low = split(b_raw * g)
            h = (dg(ones, h_high, ((1,), (1,))) + dg(ones, h_low, ((1,), (1,))))[:1]
            for d in range(NO):
                u_sum[d, j] = u[RK * d : RK * (d + 1)]
            for v in range(NO // 2):
                x = h[:, SIDE * v : SIDE * (v + 1)]
                y = jnp.concatenate([x[:, RK:], x[:, :RK]], axis=1)
                h_out[2 * v][pl.ds(j, 1), :] = jnp.where(left, x, y)
                h_out[2 * v + 1][pl.ds(j, 1), :] = jnp.where(left, y, x)
            terms.append(g * c)

        def finish(half):
            z, cols = place(js[half])
            g_sum[z, :, cols] += terms[half]
            for copy in leave(js[half]):
                copy.start()

        finish(0)
        pl.when(both)(lambda: finish(1))

    copies = [pltpu.make_async_copy(g_sum.at[z], g_out.at[z], g_sems.at[z]) for z in range(NZ)]
    for copy in copies:
        copy.start()

    @pl.loop(0, n)
    def _(j):
        for copy in leave(j):
            copy.wait()

    for copy in copies:
        copy.wait()


def hour_pack_kernel(scal, lst, h0, h1, h2, h3, hour):
    hour[...] = jnp.zeros_like(hour)
    upper = jnp.right_shift(lax.broadcasted_iota(i32, (1, SIDE), 1), 6)
    for d, h in enumerate((h0, h1, h2, h3)):

        def work(j, k):
            slot = lst[2 * LIST + k]
            g, i = jnp.right_shift(slot, 3), jnp.bitwise_and(slot, 7)
            cols = lane_block(jnp.right_shift(i, 1))
            hour[g, :, cols] += jnp.where(upper == jnp.bitwise_and(i, 1), h[pl.ds(j, 1), :], 0.0)

        each_tile(scal[0], lst, d, work)


def src_sum_kernel(scal, lst, u0, u1, u2, u3, back, keep, give):
    own, x_at, c_at = scal[0], scal[1], scal[2]
    keep[...] = jnp.zeros_like(keep)
    give[...] = jnp.zeros_like(give)
    for d, u in enumerate((u0, u1, u2, u3)):

        def work(j, k):
            src_at = lst[k]
            cols = lane_block(jnp.bitwise_and(src_at, STORED - 1))
            dx = jnp.bitwise_and(jnp.right_shift(src_at, 5) - x_at, NX - 1)
            dc = jnp.bitwise_and(jnp.right_shift(src_at, 4) + c_at, NC - 1)
            for sc, total in enumerate((keep, give)):

                @pl.when(dc == sc)
                def _():
                    total[dx, :, cols] += u[j]

        each_tile(own, lst, d, work)


def stack_kernel(p0, p1, p2, p3, out):
    for d, p in enumerate((p0, p1, p2, p3)):
        out[RK * d : RK * (d + 1), :] = p[...]


def join_kernel(scal, p0, p1, p2, p3, out):
    for d, p in enumerate((p0, p1, p2, p3)):
        to = jnp.bitwise_and(scal[0] + d, NO - 1)
        out[:, pl.ds(pl.multiple_of(to * PART, PART), PART)] = p[...]


def hour_kernel(scal, hours, where, back, out, both):
    first_hour = scal[1]
    both[...] = jnp.zeros_like(both)
    upper = jnp.right_shift(lax.broadcasted_iota(i32, (1, SIDE), 1), 6)

    @pl.loop(0, TILE_CAP)
    def _(t):
        at = where[t]

        @pl.when(at >= 0)
        def _():
            slot = jnp.bitwise_and(at, 7)
            row = back[jnp.right_shift(at, 3), :, lane_block(jnp.right_shift(slot, 1))]
            both[pl.ds(hours[t] - first_hour, 1), :] += jnp.where(upper == jnp.bitwise_and(slot, 1), row, 0.0)

    out[...] = both[:, :RK] + both[:, RK:]


def shape(*dims, dtype=f32):
    return jax.ShapeDtypeStruct(dims, dtype)


def call(kernel, out_shape, in_specs, args, out_specs=None, scratch=(), vmem=24):
    if out_specs is None:
        out_specs = jax.tree.map(lambda _: VMEM, out_shape)
    return pl.pallas_call(
        kernel, out_shape=out_shape, in_specs=in_specs, out_specs=out_specs,
        scratch_shapes=scratch, compiler_params=pltpu.CompilerParams(vmem_limit_bytes=vmem * MIB),
    )(*args)


def hop(value, axis, size, by):
    if by == 0:
        return value
    return lax.ppermute(value, axis, [(i, (i + by) % size) for i in range(size)])


def per_device(
    src_factor, dst_factor, hour_factor, tile_src, tile_dst, tile_hour, tile_count, src_place, dst_place, tile_bits
):
    z_at, x_at, c_at, own = (lax.axis_index(n).astype(i32) for n in ("z", "x", "c", "own"))
    first_hour = ((z_at * NX + x_at) * NC + c_at) * hour_factor.shape[0]
    live = tile_count[0]
    half = RK // 2

    def part_of(d):
        return jnp.bitwise_and(own + d, NO - 1) * PART

    def one_round(pair_round, base, src_factor, dst_factor):
        src_factor, dst_factor, pair_round = lax.optimization_barrier((src_factor, dst_factor, pair_round))
        with jax.named_scope("slots"):
            scal = jnp.stack([own, first_hour, live, pair_round])
            sent, where = call(
                send_kernel, (shape(GROUPS, ROWS, SIDE), shape(TILE_CAP, dtype=i32)),
                [SMEM] * 6 + [VMEM] * 2,
                (scal, tile_src, tile_dst, tile_hour, src_place, dst_place, tile_bits, hour_factor),
                out_specs=(VMEM, SMEM), scratch=[pltpu.SMEM((GROUPS,), i32)],
            )
        with jax.named_scope("gather_dst"):
            parts = [
                hop(lax.dynamic_slice(dst_factor, (0, part_of(d)), (RK, PART)), "own", NO, d) for d in range(NO)
            ]
            parts, sent = lax.optimization_barrier((parts, sent))
            b_mine = call(stack_kernel, shape(RANK, PART), [VMEM] * NO, parts)
            b_all = lax.all_gather(b_mine, "z", axis=0)
        with jax.named_scope("slots"):
            got = lax.all_to_all(sent, SLAB, 0, 0)
            rows = got.reshape(GROUPS * ROWS, SIDE)
            told = got[:, ROWS - 1].astype(i32)
        with jax.named_scope("gather_src"):
            stored, _ = lax.optimization_barrier((src_factor, b_mine))
            up = hop(stored, "x", NX, 1)
            down = hop(stored, "x", NX, -1)
            far_top = hop(up[:half], "x", NX, 1)
            far_bottom = hop(down[half:], "x", NX, -1)
            mine = (stored, down, up, far_top, far_bottom)
            a_all = mine + tuple(hop(v, "c", NC, 1) for v in mine)
        at = jnp.stack([own, x_at, c_at, base])
        with jax.named_scope("list"):
            lst = call(
                list_kernel, shape(3 * LIST + 8, dtype=i32), [SMEM, VMEM], (at, got), out_specs=SMEM,
                scratch=[
                    pltpu.SMEM((NO,), i32), pltpu.VMEM((GROUPS, SIDE), i32), pltpu.SMEM((GROUPS, SIDE), i32),
                    pltpu.SemaphoreType.DMA,
                ],
            )
        with jax.named_scope("src_exchange"):
            a_out = call(
                src_pack_kernel, (shape(PER, XROWS, SIDE),) * NO, [SMEM] * 2 + [VMEM] * 11, (at, lst, rows) + a_all
            )
            a_in = [hop(v, "own", NO, d) for d, v in enumerate(a_out)]
        with jax.named_scope("tiles"):
            g_sum, *out = call(
                tile_kernel,
                (shape(NZ, RANK, PART),) + (shape(PER, RK, SIDE),) * NO + (shape(PER, SIDE),) * NO,
                [SMEM] * 2 + [VMEM] * NO + [HBM], (at, lst, *a_in, b_all), out_specs=(HBM,) * (1 + NO) + (VMEM,) * NO,
                scratch=[
                    pltpu.VMEM((PER, RANK, SIDE), f32), pltpu.VMEM((NZ, RANK, PART), f32),
                    pltpu.VMEM((NO, PER, RK, SIDE), f32), pltpu.VMEM((2, SIDE, SIDE), f32),
                    pltpu.SemaphoreType.DMA((PER,)), pltpu.SemaphoreType.DMA((NZ,)),
                    pltpu.SemaphoreType.DMA((NO, PER)),
                ],
                vmem=52,
            )
        with jax.named_scope("hours"):
            h = [hop(v, "own", NO, -d) for d, v in enumerate(out[NO:])]
            hour_terms = call(hour_pack_kernel, shape(GROUPS, 1, 3 * SIDE), [SMEM] * 2 + [VMEM] * NO, (at, lst, *h))
            back = lax.all_to_all(hour_terms, SLAB, 0, 0)
            grad_hour = call(
                hour_kernel, shape(*hour_factor.shape), [SMEM] * 3 + [VMEM], (scal, tile_hour, where, back),
                scratch=[pltpu.VMEM((hour_factor.shape[0], SIDE), f32)],
            )
        with jax.named_scope("src_back"):
            u_out, _ = lax.optimization_barrier((out[:NO], h))
            u = [hop(v, "own", NO, -d) for d, v in enumerate(u_out)]
            keep, give = call(
                src_sum_kernel, (shape(NX, RK, STORED * SIDE),) * 2, [SMEM] * 2 + [VMEM] * NO + [ANY],
                (at, lst, *u, back),
            )
            s = keep + hop(give, "c", NC, 1)
            top = hop(s[2, :half], "x", NX, 1)
            bottom = hop(s[2, half:], "x", NX, -1)
            one = hop(jnp.concatenate([s[1, :half] + top, s[1, half:]]), "x", NX, 1)
            three = hop(jnp.concatenate([s[3, :half], s[3, half:] + bottom]), "x", NX, -1)
            grad_src = s[0] + one + three
        with jax.named_scope("dst_back"):
            g_part = lax.psum_scatter(g_sum, "z", scatter_dimension=0)
            pieces = [hop(g_part[RK * d : RK * (d + 1)], "own", NO, -d) for d in range(NO)]
            grad_dst = call(join_kernel, shape(*dst_factor.shape), [SMEM] + [VMEM] * NO, (at, *pieces))
        return (grad_src, grad_dst, grad_hour), told

    zero = jnp.zeros((), i32)
    grads, told = one_round(zero, zero, src_factor, dst_factor)

    src_at, dst_at, rank = (told[:, 32 * i : 32 * i + TILE_CAP].reshape(-1) for i in range(1, 4))
    worker = (src_at // 128) * 32 + (dst_at // STORED) % 8 * NO + dst_at % STORED // NO
    alive = src_at >= 0

    def busiest(pair_round):
        here = alive & (rank // SLOTS == pair_round)
        counts = jnp.sum((worker[None, :] == jnp.arange(GROUPS * NO, dtype=i32)[:, None]) & here[None, :], axis=1)
        return jnp.max(counts.astype(i32))

    def following(pair_round, base):
        more = base + PER < busiest(pair_round)
        return jnp.where(more, pair_round, pair_round + 1), jnp.where(more, base + PER, 0)

    def body(state):
        pair_round, base, sums = state
        terms, _ = one_round(pair_round, base, src_factor, dst_factor)
        return following(pair_round, base) + (jax.tree.map(jnp.add, sums, terms),)

    top_rank = jnp.max(jnp.where(alive, rank, -1))
    last = lax.while_loop(lambda state: top_rank >= state[0] * SLOTS, body, following(zero, zero) + (grads,))
    return last[2]


def solution(mesh):
    fine = Mesh(mesh.devices.reshape(NZ, NX, NC, NO), SLAB + ("own",))
    return jax.shard_map(
        per_device,
        mesh=fine,
        in_specs=(
            P("own", SLAB), P("own", SLAB), P(SLAB, "own"), P(SLAB), P(SLAB), P(SLAB), P(SLAB), P(), P(),
            P(SLAB, None, None),
        ),
        out_specs=(P("own", SLAB), P("own", SLAB), P(SLAB, "own")),
        check_vma=False,
    )
```

```python
import jax
import jax.numpy as jnp
from jax import lax
from jax.experimental import pallas as pl
from jax.experimental.pallas import tpu as pltpu
from jax.sharding import Mesh, PartitionSpec as P

NZ, NX, NC, NO = 8, 4, 2, 4
SLAB = ("z", "x", "c")
GROUPS = 64
TILE_CAP = 30
SIDE = 128
RK = 64
RANK = RK * NO
STORED = 16
PART = STORED // NO * SIDE
SLOTS = 5
ROWS = 3 * SLOTS + 1
PER = 15
LIST = NO * PER
XROWS = RK + 8
VMEM = pl.BlockSpec(memory_space=pltpu.VMEM)
SMEM = pl.BlockSpec(memory_space=pltpu.SMEM)
ANY = pl.BlockSpec(memory_space=pl.ANY)
HBM = pl.BlockSpec(memory_space=pltpu.HBM)
f32, bf16, i32 = jnp.float32, jnp.bfloat16, jnp.int32
MIB = 1024 * 1024


def lane_block(within):
    return pl.ds(pl.multiple_of(within * SIDE, SIDE), SIDE)


def split(x):
    hi = x.astype(bf16)
    return hi, (x - hi.astype(f32)).astype(bf16)


def dot3(a, b, dims):
    dg = lambda p, q: lax.dot_general(p, q, (dims, ((), ())), preferred_element_type=f32)
    return dg(a[0], b[0]) + (dg(a[0], b[1]) + dg(a[1], b[0]))


def as_column(row):
    return jnp.broadcast_to(row, (SIDE, RK)).T


def send_kernel(scal, src_ids, dst_ids, hours, src_place, dst_place, bits, hour_rows, out, where, count):
    own, first_hour, live, pair_round = scal[0], scal[1], scal[2], scal[3]

    @pl.loop(0, GROUPS)
    def _(g):
        count[g] = 0

    out[...] = jnp.zeros_like(out)
    lane = lax.broadcasted_iota(i32, (1, SIDE), 1)

    def step(t, told):
        src_at = src_place[src_ids[t]]
        dst_at = dst_place[dst_ids[t]]
        to = jnp.right_shift(src_at, 7) * 8 + jnp.bitwise_and(jnp.right_shift(dst_at, 4), 7)
        rank = count[to]
        slot = rank - pair_round * SLOTS
        here = (t < live) & (slot >= 0) & (slot < SLOTS)
        where[t] = jnp.where(here, to * 8 + slot, -1)

        @pl.when(t < live)
        def _():
            count[to] = rank + 1

        @pl.when(here)
        def _():
            for i in range(2):
                out[to, pl.ds(3 * slot + i, 1), :] = bits[t, pl.ds(2 * own + i, 1), :].astype(f32)
            out[to, pl.ds(3 * slot + 2, 1), :RK] = hour_rows[pl.ds(hours[t] - first_hour, 1), :]
            row = out[to, ROWS - 1 : ROWS, :]
            row = jnp.where(lane == slot, src_at.astype(f32), row)
            row = jnp.where(lane == 8 + slot, dst_at.astype(f32), row)
            out[to, ROWS - 1 : ROWS, :] = jnp.where(lane == 16, (slot + 1).astype(f32), row)

        alive = t < live
        told = jnp.where(lane == t + 32, jnp.where(alive, src_at, -1).astype(f32), told)
        told = jnp.where(lane == t + 64, dst_at.astype(f32), told)
        return jnp.where(lane == t + 96, rank.astype(f32), told)

    told = lax.fori_loop(0, TILE_CAP, step, jnp.zeros((1, SIDE), f32))
    out[:, ROWS - 1 : ROWS, :] += jnp.broadcast_to(told[None], (GROUPS, 1, SIDE))


def list_kernel(scal, got, lst, seen, staged, meta, sem):
    base = scal[3]
    for o in range(NO):
        seen[o] = 0
    staged[...] = got[:, ROWS - 1, :].astype(i32)
    copy = pltpu.make_async_copy(staged, meta, sem)
    copy.start()
    copy.wait()

    @pl.loop(0, GROUPS)
    def _(g):
        @pl.loop(0, meta[g, 16])
        def _(i):
            dst_at = meta[g, 8 + i]
            to = jnp.bitwise_and(jnp.right_shift(dst_at, 2), NO - 1)
            pos = seen[to] - base
            seen[to] += 1

            @pl.when((pos >= 0) & (pos < PER))
            def _():
                at = to * PER + pos
                lst[at] = meta[g, i]
                lst[LIST + at] = dst_at
                lst[2 * LIST + at] = g * 8 + i

    for o in range(NO):
        lst[3 * LIST + o] = jnp.clip(seen[o] - base, 0, PER)


def each_tile(own, lst, d, work):
    to = jnp.bitwise_and(own + d, NO - 1)

    @pl.loop(0, lst[3 * LIST + to])
    def _(j):
        work(j, PER * to + j)


def slot_row(slot):
    return jnp.right_shift(slot, 3) * ROWS + 3 * jnp.bitwise_and(slot, 7)


def src_pack_kernel(scal, lst, recv, a00, a10, a30, a2t0, a2b0, a01, a11, a31, a2t1, a2b1, *outs):
    own, x_at, c_at = scal[0], scal[1], scal[2]
    sources = (
        ((a00,), (a01,)), ((a10,), (a11,)), ((a2t0, a2b0), (a2t1, a2b1)), ((a30,), (a31,)),
    )
    for d in range(NO):

        def work(j, k):
            src_at = lst[k]
            row = slot_row(lst[2 * LIST + k])
            cols = lane_block(jnp.bitwise_and(src_at, STORED - 1))
            dx = jnp.bitwise_and(jnp.right_shift(src_at, 5) - x_at, NX - 1)
            dc = jnp.bitwise_and(jnp.right_shift(src_at, 4) + c_at, NC - 1)
            for sx in range(NX):
                for sc in range(NC):

                    @pl.when((dx == sx) & (dc == sc))
                    def _():
                        refs = sources[sx][sc]
                        step = RK // len(refs)
                        for h, ref in enumerate(refs):
                            outs[d][j, h * step : (h + 1) * step, :] = ref[:, cols]

            for i in range(3):
                outs[d][j, RK + i : RK + i + 1, :] = recv[pl.ds(row + i, 1), :]

        each_tile(own, lst, d, work)


def tile_kernel(
    scal, lst, a0, a1, a2, a3, b_all, g_out, u0, u1, u2, u3, h0, h1, h2, h3,
    blocks, g_sum, u_sum, entries, in_sems, g_sems, u_sems,
):
    own = scal[0]
    a_in, u_out, h_out = (a0, a1, a2, a3), (u0, u1, u2, u3), (h0, h1, h2, h3)
    n = lst[3 * LIST + own]
    shift = jnp.bitwise_and(lax.broadcasted_iota(i32, (32, SIDE), 0), 15)
    left = lax.broadcasted_iota(i32, (1, SIDE), 1) < RK
    ones = jnp.ones((8, SIDE), bf16)
    dg = lambda p, q, dims: lax.dot_general(p, q, (dims, ((), ())), preferred_element_type=f32)

    def place(j):
        dst_at = lst[LIST + PER * own + j]
        return jnp.right_shift(dst_at, 7), lane_block(jnp.bitwise_and(dst_at, STORED // NO - 1))

    def fetch(j):
        z, cols = place(j)
        return pltpu.make_async_copy(b_all.at[z, :, cols], blocks.at[j], in_sems.at[j])

    def leave(j):
        return [pltpu.make_async_copy(u_sum.at[d, j], u_out[d].at[j], u_sems.at[d, j]) for d in range(NO)]

    @pl.loop(0, n)
    def _(j):
        fetch(j).start()

    g_sum[...] = jnp.zeros_like(g_sum)
    @pl.loop(0, jnp.right_shift(n + 1, 1))
    def _(pair):
        js = 2 * pair, jnp.minimum(2 * pair + 1, PER - 1)
        both = 2 * pair + 1 < n
        fetch(js[0]).wait()

        @pl.when(both)
        def _():
            fetch(js[1]).wait()

        terms = []
        for half, j in enumerate(js):
            a_high, a_low = split(jnp.concatenate([a_in[d][j, :RK] for d in range(NO)], axis=0))
            c = jnp.concatenate([as_column(a_in[d][j, RK + 2 : RK + 3, :RK]) for d in range(NO)], axis=0)
            for d in range(NO):
                rows = pl.ds(pl.multiple_of(jnp.bitwise_and(own - d, NO - 1) * 32, 32), 32)
                words = jnp.concatenate(
                    [jnp.broadcast_to(a_in[d][j, RK + i : RK + i + 1, :], (16, SIDE)) for i in range(2)], axis=0
                ).astype(i32)
                entries[half, rows, :] = jnp.bitwise_and(jnp.right_shift(words, shift), 1).astype(f32)
            b_raw = blocks[j]
            b_high, b_low = split(b_raw * c)
            logits = dot3((a_high, a_low), (b_high, b_low), ((0,), (0,)))
            r_high, r_low = split(jax.nn.sigmoid(logits) - entries[half])
            u = dg(
                jnp.concatenate([b_high, b_low], axis=1), jnp.concatenate([r_high, r_high], axis=1), ((1,), (1,))
            ) + dg(b_high, r_low, ((1,), (1,)))
            g = dg(
                jnp.concatenate([a_high, a_low], axis=1), jnp.concatenate([r_high, r_high], axis=0), ((1,), (0,))
            ) + dg(a_high, r_low, ((1,), (0,)))
            h_high, h_low = split(b_raw * g)
            h = (dg(ones, h_high, ((1,), (1,))) + dg(ones, h_low, ((1,), (1,))))[:1]
            for d in range(NO):
                u_sum[d, j] = u[RK * d : RK * (d + 1)]
            for v in range(NO // 2):
                x = h[:, SIDE * v : SIDE * (v + 1)]
                y = jnp.concatenate([x[:, RK:], x[:, :RK]], axis=1)
                h_out[2 * v][pl.ds(j, 1), :] = jnp.where(left, x, y)
                h_out[2 * v + 1][pl.ds(j, 1), :] = jnp.where(left, y, x)
            terms.append(g * c)

        def finish(half):
            z, cols = place(js[half])
            g_sum[z, :, cols] += terms[half]
            for copy in leave(js[half]):
                copy.start()

        finish(0)
        pl.when(both)(lambda: finish(1))

    copies = [pltpu.make_async_copy(g_sum.at[z], g_out.at[z], g_sems.at[z]) for z in range(NZ)]
    for copy in copies:
        copy.start()

    @pl.loop(0, n)
    def _(j):
        for copy in leave(j):
            copy.wait()

    for copy in copies:
        copy.wait()


def hour_pack_kernel(scal, lst, h0, h1, h2, h3, hour):
    hour[...] = jnp.zeros_like(hour)
    upper = jnp.right_shift(lax.broadcasted_iota(i32, (1, SIDE), 1), 6)
    for d, h in enumerate((h0, h1, h2, h3)):

        def work(j, k):
            slot = lst[2 * LIST + k]
            g, i = jnp.right_shift(slot, 3), jnp.bitwise_and(slot, 7)
            cols = lane_block(jnp.right_shift(i, 1))
            hour[g, :, cols] += jnp.where(upper == jnp.bitwise_and(i, 1), h[pl.ds(j, 1), :], 0.0)

        each_tile(scal[0], lst, d, work)


def src_sum_kernel(scal, lst, u0, u1, u2, u3, back, keep, give):
    own, x_at, c_at = scal[0], scal[1], scal[2]
    keep[...] = jnp.zeros_like(keep)
    give[...] = jnp.zeros_like(give)
    for d, u in enumerate((u0, u1, u2, u3)):

        def work(j, k):
            src_at = lst[k]
            cols = lane_block(jnp.bitwise_and(src_at, STORED - 1))
            dx = jnp.bitwise_and(jnp.right_shift(src_at, 5) - x_at, NX - 1)
            dc = jnp.bitwise_and(jnp.right_shift(src_at, 4) + c_at, NC - 1)
            for sc, total in enumerate((keep, give)):

                @pl.when(dc == sc)
                def _():
                    total[dx, :, cols] += u[j]

        each_tile(own, lst, d, work)


def stack_kernel(p0, p1, p2, p3, out):
    for d, p in enumerate((p0, p1, p2, p3)):
        out[RK * d : RK * (d + 1), :] = p[...]


def join_kernel(scal, p0, p1, p2, p3, out):
    for d, p in enumerate((p0, p1, p2, p3)):
        to = jnp.bitwise_and(scal[0] + d, NO - 1)
        out[:, pl.ds(pl.multiple_of(to * PART, PART), PART)] = p[...]


def hour_kernel(scal, hours, where, back, out, both):
    first_hour = scal[1]
    both[...] = jnp.zeros_like(both)
    upper = jnp.right_shift(lax.broadcasted_iota(i32, (1, SIDE), 1), 6)

    @pl.loop(0, TILE_CAP)
    def _(t):
        at = where[t]

        @pl.when(at >= 0)
        def _():
            slot = jnp.bitwise_and(at, 7)
            row = back[jnp.right_shift(at, 3), :, lane_block(jnp.right_shift(slot, 1))]
            both[pl.ds(hours[t] - first_hour, 1), :] += jnp.where(upper == jnp.bitwise_and(slot, 1), row, 0.0)

    out[...] = both[:, :RK] + both[:, RK:]


def plan_kernel(scal, got, recv, *rest):
    sources, lst, outs, scratch = rest[:10], rest[10], rest[11 : 11 + NO], rest[11 + NO :]
    list_kernel(scal, got, lst, *scratch)
    src_pack_kernel(scal, lst, recv, *sources, *outs)


def shape(*dims, dtype=f32):
    return jax.ShapeDtypeStruct(dims, dtype)


def call(kernel, out_shape, in_specs, args, out_specs=None, scratch=(), vmem=24):
    if out_specs is None:
        out_specs = jax.tree.map(lambda _: VMEM, out_shape)
    return pl.pallas_call(
        kernel, out_shape=out_shape, in_specs=in_specs, out_specs=out_specs,
        scratch_shapes=scratch, compiler_params=pltpu.CompilerParams(vmem_limit_bytes=vmem * MIB),
    )(*args)


def hop(value, axis, size, by):
    if by == 0:
        return value
    return lax.ppermute(value, axis, [(i, (i + by) % size) for i in range(size)])


def per_device(
    src_factor, dst_factor, hour_factor, tile_src, tile_dst, tile_hour, tile_count, src_place, dst_place, tile_bits
):
    z_at, x_at, c_at, own = (lax.axis_index(n).astype(i32) for n in ("z", "x", "c", "own"))
    first_hour = ((z_at * NX + x_at) * NC + c_at) * hour_factor.shape[0]
    live = tile_count[0]
    half = RK // 2

    def part_of(d):
        return jnp.bitwise_and(own + d, NO - 1) * PART

    def one_round(pair_round, base, src_factor, dst_factor):
        src_factor, dst_factor, pair_round = lax.optimization_barrier((src_factor, dst_factor, pair_round))
        with jax.named_scope("slots"):
            scal = jnp.stack([own, first_hour, live, pair_round])
            sent, where = call(
                send_kernel, (shape(GROUPS, ROWS, SIDE), shape(TILE_CAP, dtype=i32)),
                [SMEM] * 6 + [VMEM] * 2,
                (scal, tile_src, tile_dst, tile_hour, src_place, dst_place, tile_bits, hour_factor),
                out_specs=(VMEM, SMEM), scratch=[pltpu.SMEM((GROUPS,), i32)],
            )
        with jax.named_scope("gather_dst"):
            parts = [
                hop(lax.dynamic_slice(dst_factor, (0, part_of(d)), (RK, PART)), "own", NO, d) for d in range(NO)
            ]
            parts, sent = lax.optimization_barrier((parts, sent))
            b_mine = call(stack_kernel, shape(RANK, PART), [VMEM] * NO, parts)
            b_all = lax.all_gather(b_mine, "z", axis=0)
        with jax.named_scope("slots"):
            got = lax.all_to_all(sent, SLAB, 0, 0)
            rows = got.reshape(GROUPS * ROWS, SIDE)
            told = got[:, ROWS - 1].astype(i32)
        with jax.named_scope("gather_src"):
            stored, _ = lax.optimization_barrier((src_factor, b_mine))
            up = hop(stored, "x", NX, 1)
            down = hop(stored, "x", NX, -1)
            far_top = hop(up[:half], "x", NX, 1)
            far_bottom = hop(down[half:], "x", NX, -1)
            mine = (stored, down, up, far_top, far_bottom)
            a_all = mine + tuple(hop(v, "c", NC, 1) for v in mine)
        at = jnp.stack([own, x_at, c_at, base])
        with jax.named_scope("src_exchange"):
            lst, *a_out = call(
                plan_kernel, (shape(3 * LIST + 8, dtype=i32),) + (shape(PER, XROWS, SIDE),) * NO,
                [SMEM] + [VMEM] * 12, (at, got, rows) + a_all, out_specs=(SMEM,) + (VMEM,) * NO,
                scratch=[
                    pltpu.SMEM((NO,), i32), pltpu.VMEM((GROUPS, SIDE), i32), pltpu.SMEM((GROUPS, SIDE), i32),
                    pltpu.SemaphoreType.DMA,
                ],
            )
            a_in = [hop(v, "own", NO, d) for d, v in enumerate(a_out)]
        with jax.named_scope("tiles"):
            g_sum, *out = call(
                tile_kernel,
                (shape(NZ, RANK, PART),) + (shape(PER, RK, SIDE),) * NO + (shape(PER, SIDE),) * NO,
                [SMEM] * 2 + [VMEM] * NO + [HBM], (at, lst, *a_in, b_all), out_specs=(HBM,) * (1 + NO) + (VMEM,) * NO,
                scratch=[
                    pltpu.VMEM((PER, RANK, SIDE), f32), pltpu.VMEM((NZ, RANK, PART), f32),
                    pltpu.VMEM((NO, PER, RK, SIDE), f32), pltpu.VMEM((2, SIDE, SIDE), f32),
                    pltpu.SemaphoreType.DMA((PER,)), pltpu.SemaphoreType.DMA((NZ,)),
                    pltpu.SemaphoreType.DMA((NO, PER)),
                ],
                vmem=52,
            )
        with jax.named_scope("hours"):
            h = [hop(v, "own", NO, -d) for d, v in enumerate(out[NO:])]
            hour_terms = call(hour_pack_kernel, shape(GROUPS, 1, 3 * SIDE), [SMEM] * 2 + [VMEM] * NO, (at, lst, *h))
            back = lax.all_to_all(hour_terms, SLAB, 0, 0)
            grad_hour = call(
                hour_kernel, shape(*hour_factor.shape), [SMEM] * 3 + [VMEM], (scal, tile_hour, where, back),
                scratch=[pltpu.VMEM((hour_factor.shape[0], SIDE), f32)],
            )
        with jax.named_scope("src_back"):
            u_out, _ = lax.optimization_barrier((out[:NO], h))
            u = [hop(v, "own", NO, -d) for d, v in enumerate(u_out)]
            keep, give = call(
                src_sum_kernel, (shape(NX, RK, STORED * SIDE),) * 2, [SMEM] * 2 + [VMEM] * NO + [ANY],
                (at, lst, *u, back),
            )
            s = keep + hop(give, "c", NC, 1)
            top = hop(s[2, :half], "x", NX, 1)
            bottom = hop(s[2, half:], "x", NX, -1)
            one = hop(jnp.concatenate([s[1, :half] + top, s[1, half:]]), "x", NX, 1)
            three = hop(jnp.concatenate([s[3, :half], s[3, half:] + bottom]), "x", NX, -1)
            grad_src = s[0] + one + three
        with jax.named_scope("dst_back"):
            g_part = lax.psum_scatter(g_sum, "z", scatter_dimension=0)
            pieces = [hop(g_part[RK * d : RK * (d + 1)], "own", NO, -d) for d in range(NO)]
            grad_dst = call(join_kernel, shape(*dst_factor.shape), [SMEM] + [VMEM] * NO, (at, *pieces))
        return (grad_src, grad_dst, grad_hour), told

    zero = jnp.zeros((), i32)
    grads, told = one_round(zero, zero, src_factor, dst_factor)

    src_at, dst_at, rank = (told[:, 32 * i : 32 * i + TILE_CAP].reshape(-1) for i in range(1, 4))
    worker = (src_at // 128) * 32 + (dst_at // STORED) % 8 * NO + dst_at % STORED // NO
    alive = src_at >= 0

    def busiest(pair_round):
        here = alive & (rank // SLOTS == pair_round)
        counts = jnp.sum((worker[None, :] == jnp.arange(GROUPS * NO, dtype=i32)[:, None]) & here[None, :], axis=1)
        return jnp.max(counts.astype(i32))

    def following(pair_round, base):
        more = base + PER < busiest(pair_round)
        return jnp.where(more, pair_round, pair_round + 1), jnp.where(more, base + PER, 0)

    def body(state):
        pair_round, base, sums = state
        terms, _ = one_round(pair_round, base, src_factor, dst_factor)
        return following(pair_round, base) + (jax.tree.map(jnp.add, sums, terms),)

    top_rank = jnp.max(jnp.where(alive, rank, -1))
    last = lax.while_loop(lambda state: top_rank >= state[0] * SLOTS, body, following(zero, zero) + (grads,))
    return last[2]


def solution(mesh):
    fine = Mesh(mesh.devices.reshape(NZ, NX, NC, NO), SLAB + ("own",))
    return jax.shard_map(
        per_device,
        mesh=fine,
        in_specs=(
            P("own", SLAB), P("own", SLAB), P(SLAB, "own"), P(SLAB), P(SLAB), P(SLAB), P(SLAB), P(), P(),
            P(SLAB, None, None),
        ),
        out_specs=(P("own", SLAB), P("own", SLAB), P(SLAB, "own")),
        check_vma=False,
    )
```
